128 devices in a mesh: slab: 32 (over y, z, core), sub: 4 (over x).
Axes of the slice: x: 4, y: 4, z: 4, core: 2. Of those that a mesh axis runs over, the one named last changes fastest.
Arguments:
- features: bfloat16 [512, 64, 96, 128], P('slab', 'sub'), may hold values from -6 to 6
- voxel_mask: int32 [512, 64, 128], P('slab', 'sub'), may hold values from 0 to 1, as said below
- weight: bfloat16 [27, 96, 96], replicated, may hold values from -0.125 to 0.125
- norm_gain: float32 [96], replicated, may hold values from 0.5 to 1.5
- norm_bias: float32 [96], replicated, may hold values from -1 to 1
- out_grad: bfloat16 [512, 64, 96, 128], P('slab', 'sub'), may hold values from -6 to 6
Outputs:
- normed_out: bfloat16 [512, 64, 96, 128], P('slab', 'sub')
- feature_grad: bfloat16 [512, 64, 96, 128], P('slab', 'sub')
- weight_grad: float32 [27, 96, 96], replicated
- gain_grad: float32 [96], replicated
- bias_grad: float32 [96], replicated
The draws below stay inside these ranges and needn't reach their ends.
Inputs may be any that keep to these rules, and one draw needn't show every extreme that they name: `voxel_mask`: the grid is cut into pillars of 8 x 8 x 128 voxels aligned to multiples of 8 along x and y. For every two devices with sub indices 2k and 2k+1 and the same slab index, exactly two of their pillars hold active voxels; one device holds at most 2 of them, and some device holds 2.
All inputs are finite; a program needn't handle non-finite values.
Results may differ from the reference program's by a relative error of at most 0.0049.
Values may be sent and summed in bfloat16 or wider, within the bound.
No kernel may reach another device: no remote copies, remote signals or barrier semaphores. Data moves between devices by JAX's collectives and lax.ppermute only.
A program may use at most 384 MiB of HBM per device.

```python
import jax
import jax.numpy as jnp
from jax import lax

C = 96
BRICK = 8
TAPS = 27
PX = 2
PY = 2
NZ = 128
NX = 512
NY = 64
PILLARS = 128


def draw_voxel_mask(key, part):
    key = jax.random.fold_in(key, 11)
    slabs = NX // (PX * BRICK)
    subs = NY // (PY * BRICK)
    pairs = slabs * (subs // 2)
    count_key, force_key, order_key, level_key, voxel_key = jax.random.split(key, 5)
    first = jax.random.randint(count_key, (pairs,), 0, 3)
    forced = jax.random.randint(force_key, (), 0, pairs)
    first = jnp.where(jnp.arange(pairs) == forced, 2, first)
    counts = jnp.stack([first, 2 - first], axis=-1).reshape(slabs, subs)
    ranks = jax.vmap(lambda single: jax.random.permutation(single, PX * PY))(jax.random.split(order_key, slabs * subs))
    occupied = (ranks.reshape(slabs, subs, PX, PY) < counts[:, :, None, None]).astype(jnp.int32)
    pillars = occupied.transpose(0, 2, 1, 3).reshape(slabs * PX, subs * PY)
    pillars = jnp.repeat(jnp.repeat(pillars, BRICK, axis=0), BRICK, axis=1)
    levels = jax.random.randint(level_key, (NX // BRICK, NY // BRICK, NZ // BRICK), 20, 90)
    levels = jnp.repeat(jnp.repeat(jnp.repeat(levels, BRICK, axis=0), BRICK, axis=1), BRICK, axis=2)
    voxels = jax.random.randint(voxel_key, (NX, NY, NZ), 0, 100)
    xpos = jnp.arange(NX)[:, None, None]
    ypos = jnp.arange(NY)[None, :, None]
    zpos = jnp.arange(NZ)[None, None, :]
    corner = (xpos % BRICK == 0) & (ypos % BRICK == 0) & (zpos == 0)
    active = (voxels < levels) | corner
    return active.astype(jnp.int32) * pillars[:, :, None]


def shard_levels(rng, extent, pieces, low, high):
    def one(axis_at, shards_of):
        heights = jax.random.uniform(jax.random.fold_in(jax.random.fold_in(rng, 6), axis_at), (shards_of,), jnp.float32, low / len(pieces), high / len(pieces))
        return jnp.repeat(jnp.exp(heights), extent[axis_at] // shards_of).reshape((-1,) + (1,) * (len(extent) - axis_at - 1))

    factor_of = one(*pieces[0])
    for cut in pieces[1:]:
        factor_of = factor_of * one(*cut)
    return factor_of


def scatter_about(key, extent, spread, bound, pieces=(), held_as=jnp.bfloat16):
    drawn = spread * jax.random.normal(key, extent, jnp.float32)
    if pieces:
        drawn = drawn * shard_levels(key, extent, pieces, -0.22, 0.18)
    return jnp.clip(drawn, -bound, bound).astype(held_as)


def setup_inputs(seed: int = 0) -> dict:
    arg_keys = jax.random.split(jax.random.key(seed), 7)
    features = scatter_about(arg_keys[0], (NX, NY, C, NZ), 1.0, 6.0, ((0, 32), (1, 4)))
    voxel_mask = draw_voxel_mask(jax.random.fold_in(arg_keys[6], 71), 0)
    weight = scatter_about(arg_keys[2], (TAPS, C, C), (TAPS * C) ** -0.5, 0.125)
    norm_gain = jnp.clip(1.0 + 0.1 * jax.random.normal(arg_keys[3], (C,), jnp.float32), 0.5, 1.5)
    norm_bias = jnp.clip(jax.random.uniform(arg_keys[4], (C,), jnp.float32, -1.0, 1.0), -1.0, 1.0)
    out_grad = scatter_about(arg_keys[5], (NX, NY, C, NZ), 1.0, 6.0, ((0, 32), (1, 4)))
    return dict(features=features, voxel_mask=voxel_mask, weight=weight, norm_gain=norm_gain, norm_bias=norm_bias, out_grad=out_grad)


EPSILON = 1e-05

def tap_offsets():
    return [(i, j, k) for i in range(3) for j in range(3) for k in range(3)]

def reference(features, voxel_mask, weight, norm_gain, norm_bias, out_grad):
    mask_bf = voxel_mask.astype(jnp.bfloat16)
    masked = features * mask_bf[:, :, None, :]
    padded = jnp.pad(masked, ((1, 1), (1, 1), (0, 0), (1, 1)))
    across = NX // BRICK
    along = NY // BRICK
    flags = voxel_mask.reshape(across, BRICK, along, BRICK, NZ).max(axis=(1, 3, 4)).reshape(-1)
    order = jnp.argsort(-flags, stable=True)[:PILLARS].astype(jnp.int32)
    rows = (order // along * BRICK).astype(jnp.int32)
    cols = (order % along * BRICK).astype(jnp.int32)
    weight32 = weight.astype(jnp.float32)
    span = BRICK + 2
    zero = jnp.int32(0)
    highest = lax.Precision.HIGHEST

    def block(field, row, col, size):
        return lax.dynamic_slice(field, (row, col) + (zero,) * (field.ndim - 2), (size, size) + field.shape[2:])

    def forward(start):
        row, col = start
        patch = block(padded, row, col, span).astype(jnp.float32)
        weights_f = block(mask_bf, row, col, BRICK).astype(jnp.float32)[:, :, None, :]
        total = jnp.zeros((BRICK, BRICK, C, NZ), jnp.float32)
        for tap, (i, j, k) in enumerate(tap_offsets()):
            piece = patch[i:i + BRICK, j:j + BRICK, :, k:k + NZ]
            total = total + jnp.einsum('oc,xycz->xyoz', weight32[tap], piece, precision=highest)
        upstream = block(out_grad, row, col, BRICK).astype(jnp.float32) * weights_f
        return (total * weights_f, weights_f, upstream)
    conv_out, weights_f, upstream = lax.map(forward, (rows, cols))
    count = jnp.sum(weights_f)
    total = lax.optimization_barrier(jnp.sum(conv_out, axis=(0, 1, 2, 4)))
    squares = lax.optimization_barrier(jnp.sum(conv_out * conv_out, axis=(0, 1, 2, 4)))
    mean = total / count
    inv_std = lax.rsqrt(squares / count - mean * mean + EPSILON)
    normed = (conv_out - mean[:, None]) * inv_std[:, None] * weights_f
    y_blocks = ((norm_gain[:, None] * normed + norm_bias[:, None]) * weights_f).astype(jnp.bfloat16)
    bias_grad = lax.optimization_barrier(jnp.sum(upstream, axis=(0, 1, 2, 4)))
    gain_grad = lax.optimization_barrier(jnp.sum(upstream * normed, axis=(0, 1, 2, 4)))
    scaled = (norm_gain * inv_std)[:, None]
    dh_blocks = (scaled * (upstream - (bias_grad / count)[:, None] - normed * (gain_grad / count)[:, None]) * weights_f).astype(jnp.bfloat16)

    def add_weight(carry, item):
        row, col, grads = item
        patch = block(padded, row, col, span).astype(jnp.float32)
        grads32 = grads.astype(jnp.float32)
        terms = jnp.stack([jnp.einsum('xyoz,xycz->oc', grads32, patch[i:i + BRICK, j:j + BRICK, :, k:k + NZ], precision=highest) for i, j, k in tap_offsets()])
        return (carry + terms, None)
    weight_grad, _ = lax.scan(add_weight, jnp.zeros((TAPS, C, C), jnp.float32), (rows, cols, dh_blocks))

    def place(blocks):

        def put(index, field):
            return lax.dynamic_update_slice(field, blocks[index], (rows[index], cols[index], zero, zero))
        return lax.fori_loop(0, PILLARS, put, jnp.zeros((NX, NY, C, NZ), blocks.dtype))
    dh_dense = place(dh_blocks)
    grad_pad = jnp.pad(dh_dense, ((1, 1), (1, 1), (0, 0), (1, 1)))

    def backward(item):
        row, col, weights_one = item
        patch = block(grad_pad, row, col, span).astype(jnp.float32)
        total = jnp.zeros((BRICK, BRICK, C, NZ), jnp.float32)
        for tap, (i, j, k) in enumerate(tap_offsets()):
            piece = patch[2 - i:2 - i + BRICK, 2 - j:2 - j + BRICK, :, 2 - k:2 - k + NZ]
            total = total + jnp.einsum('oc,xyoz->xycz', weight32[tap], piece, precision=highest)
        return (total * weights_one).astype(jnp.bfloat16)
    dx_blocks = lax.map(backward, (rows, cols, weights_f))
    return (place(y_blocks), place(dx_blocks), weight_grad, gain_grad, bias_grad)
```

```python
import functools

import jax
import jax.numpy as jnp
from jax import lax
from jax.experimental import pallas as pl
from jax.experimental.pallas import tpu as pltpu
from jax.sharding import PartitionSpec as P

BRICK = 8
SLOTS = 2
EPSILON = 1e-05
DEVICES = 128
CHANS = 96
DEPTH = 128
TILES = 7
ROWS = 3 * CHANS
COLS = TILES * DEPTH
F32 = jnp.float32
BF16 = jnp.bfloat16
VMEM_LIMIT = 56 * 1024 * 1024

ANY = pl.BlockSpec(memory_space=pl.ANY)
VMEM = pl.BlockSpec(memory_space=pltpu.VMEM)
SMEM = pl.BlockSpec(memory_space=pltpu.SMEM)


def slot_table(voxel_mask):
    across = voxel_mask.shape[0] // BRICK
    along = voxel_mask.shape[1] // BRICK
    flags = (
        voxel_mask.reshape(across, BRICK, along, BRICK, voxel_mask.shape[2])
        .max(axis=(1, 3, 4))
        .reshape(-1)
    )
    before = jnp.cumsum(flags) - flags
    position = jnp.arange(flags.shape[0], dtype=jnp.int32)
    occupied = jnp.sum(flags)
    rank = jnp.where(flags == 1, before, occupied + position - before)
    order = jnp.sum(jnp.where(rank[None, :] == position[:, None], position[None, :], 0), axis=1)
    table = jnp.stack([order // along * BRICK, order % along * BRICK], axis=1).reshape(-1)
    return jnp.concatenate([table, occupied[None]]).astype(jnp.int32)


def corner(meta, slot):
    return (pl.multiple_of(meta[2 * slot], BRICK), pl.multiple_of(meta[2 * slot + 1], BRICK))


def rim_copies(rims, field, sems):
    xm, xp, ym, yp = rims
    return [
        pltpu.make_async_copy(xm, field.at[0, pl.ds(1, 16)], sems.at[0]),
        pltpu.make_async_copy(xp, field.at[17, pl.ds(1, 16)], sems.at[1]),
        pltpu.make_async_copy(ym, field.at[:, 0], sems.at[2]),
        pltpu.make_async_copy(yp, field.at[:, 17], sems.at[3]),
    ]


def zero_pillars(meta, field, edge):
    occupied = meta[8]
    for slot in range(4):

        @pl.when(slot >= occupied)
        def _():
            x0, y0 = corner(meta, slot)

            def clear(row, carry):
                for col in range(BRICK):
                    field[x0 + row + edge, y0 + col + edge] = jnp.zeros((CHANS, DEPTH), field.dtype)
                return carry

            lax.fori_loop(0, BRICK, clear, 0)


def mask_pillar(meta, slot, mask, field):
    x0, y0 = corner(meta, slot)

    def apply(row, carry):
        active = mask[x0 + row, pl.ds(y0, BRICK), :]
        for col in range(BRICK):
            keep = jnp.broadcast_to(active[col : col + 1], (CHANS, DEPTH)).astype(BF16)
            at = (x0 + row + 1, y0 + col + 1)
            field[at] = field[at] * keep
        return carry

    lax.fori_loop(0, BRICK, apply, 0)


def column_convs(field, kernel_ref, x, y0, flipped):
    lane = lax.broadcasted_iota(jnp.int32, (CHANS, DEPTH), 1)
    up, down = (2, 0) if flipped else (0, 2)
    outs = []
    for pair in range(BRICK // 2):
        pieces = []
        for a in range(3):
            for b in range(3):
                col = y0 + 2 * pair + b
                pieces.append(jnp.concatenate([field[x + a, col], field[x + a, col + 1]], axis=1))
        pieces.append(jnp.zeros((COLS - 9 * CHANS, 2 * DEPTH), BF16))
        planes = jnp.dot(
            kernel_ref[...], jnp.concatenate(pieces, axis=0), preferred_element_type=F32
        )
        for half in range(2):
            part = [
                planes[CHANS * e : CHANS * (e + 1), DEPTH * half : DEPTH * (half + 1)]
                for e in range(3)
            ]
            outs.append(
                part[1]
                + jnp.where(lane == 0, 0.0, pltpu.roll(part[up], 1, 1))
                + jnp.where(lane == DEPTH - 1, 0.0, pltpu.roll(part[down], DEPTH - 1, 1))
            )
    return outs


def forward_kernel(
    meta, features, out_grad, mask, xm, xp, ym, yp, kernel_ref, conv_out, stats, field, grads, convs, sums, sem_rim, sem_in, sem_og, sem_out
):
    occupied = meta[8]
    rims = rim_copies((xm, xp, ym, yp), field, sem_rim)
    for copy in rims:
        copy.start()
    loads = []
    for slot in range(SLOTS):
        x0, y0 = corner(meta, slot)
        loads.append(
            (
                pltpu.make_async_copy(
                    features.at[pl.ds(x0, BRICK), pl.ds(y0, BRICK)],
                    field.at[pl.ds(x0 + 1, BRICK), pl.ds(y0 + 1, BRICK)],
                    sem_in.at[slot],
                ),
                pltpu.make_async_copy(
                    out_grad.at[pl.ds(x0, BRICK), pl.ds(y0, BRICK)], grads.at[slot], sem_og.at[slot]
                ),
            )
        )
    for slot in range(SLOTS):

        @pl.when(slot < occupied)
        def _():
            loads[slot][0].start()

    for slot in range(SLOTS):

        @pl.when(slot < occupied)
        def _():
            loads[slot][1].start()

    zero_pillars(meta, field, 1)
    sums[...] = jnp.zeros(sums.shape, F32)
    for copy in rims:
        copy.wait()
    for slot in range(SLOTS):

        @pl.when(slot < occupied)
        def _():
            loads[slot][0].wait()
            mask_pillar(meta, slot, mask, field)

    for slot in range(SLOTS):

        @pl.when(slot < occupied)
        def _():
            x0, y0 = corner(meta, slot)
            loads[slot][1].wait()

            def row(x, carry):
                active = mask[x0 + x, pl.ds(y0, BRICK), :]
                outs = column_convs(field, kernel_ref, x0 + x, y0, False)
                total, square, upsum, cross = [sums[k] for k in range(4)]
                for col in range(BRICK):
                    keep = active[col : col + 1]
                    conv = outs[col] * keep
                    convs[slot, x, col] = conv
                    up = grads[slot, x, col].astype(F32) * keep
                    total = total + conv
                    square = square + conv * conv
                    upsum = upsum + up
                    cross = cross + up * conv
                for k, value in enumerate((total, square, upsum, cross)):
                    sums[k] = value
                sums[4, 0:BRICK] = sums[4, 0:BRICK] + active
                pltpu.make_async_copy(
                    convs.at[slot, x], conv_out.at[slot, x], sem_out.at[slot, x]
                ).start()
                return carry

            lax.fori_loop(0, BRICK, row, 0)

    ones = jnp.ones((8, DEPTH), F32)
    stats[...] = jnp.zeros(stats.shape, F32)
    for k in range(5):
        flat = lax.dot_general(
            ones,
            sums[k],
            (((1,), (1,)), ((), ())),
            precision=lax.Precision.HIGHEST,
            preferred_element_type=F32,
        )
        stats[k : k + 1, 0:CHANS] = flat[0:1]
    for slot in range(SLOTS):

        @pl.when(slot < occupied)
        def _():
            def drain(x, carry):
                pltpu.make_async_copy(
                    convs.at[slot, x], conv_out.at[slot, x], sem_out.at[slot, x]
                ).wait()
                return carry

            lax.fori_loop(0, BRICK, drain, 0)


def forward(meta, features, out_grad, mask, rims, kernel):
    return pl.pallas_call(
        forward_kernel,
        name="forward",
        out_shape=(
            jax.ShapeDtypeStruct((SLOTS, BRICK, BRICK, CHANS, DEPTH), F32),
            jax.ShapeDtypeStruct((8, DEPTH), F32),
        ),
        in_specs=[SMEM, ANY, ANY, VMEM, ANY, ANY, ANY, ANY, VMEM],
        out_specs=(ANY, VMEM),
        scratch_shapes=[
            pltpu.VMEM((18, 18, CHANS, DEPTH), BF16),
            pltpu.VMEM((SLOTS, BRICK, BRICK, CHANS, DEPTH), BF16),
            pltpu.VMEM((SLOTS, BRICK, BRICK, CHANS, DEPTH), F32),
            pltpu.VMEM((5, CHANS, DEPTH), F32),
            pltpu.SemaphoreType.DMA((4,)),
            pltpu.SemaphoreType.DMA((SLOTS,)),
            pltpu.SemaphoreType.DMA((SLOTS,)),
            pltpu.SemaphoreType.DMA((SLOTS, BRICK)),
        ],
        compiler_params=pltpu.CompilerParams(vmem_limit_bytes=VMEM_LIMIT),
        cost_estimate=pl.CostEstimate(flops=8_200_000_000, bytes_accessed=14_000_000, transcendentals=0),
    )(meta, features, out_grad, mask, *rims, kernel)


def spread(row):
    return jnp.transpose(jnp.broadcast_to(row, (DEPTH, DEPTH)))[0:CHANS]


def norm_kernel(
    meta, totals, params, conv, out_grad, mask, normed_out, dh_out, x_low, x_high, y_low, y_high, sums_out, convs, grads, ys, dense, blank, sem_conv, sem_og, sem_y, sem_dh, sem_zero, sem_rim
):
    occupied = meta[8]

    def conv_copy(slot, x):
        return pltpu.make_async_copy(conv.at[slot, x], convs.at[slot, x], sem_conv.at[slot, x])

    def og_copy(slot, x):
        x0, y0 = corner(meta, slot)
        return pltpu.make_async_copy(
            out_grad.at[x0 + x, pl.ds(y0, BRICK)], grads.at[slot, x], sem_og.at[slot, x]
        )

    def y_copy(slot, x):
        x0, y0 = corner(meta, slot)
        return pltpu.make_async_copy(
            ys.at[slot, x], normed_out.at[x0 + x, pl.ds(y0, BRICK)], sem_y.at[slot, x]
        )

    def dh_copy(slot, x):
        x0, y0 = corner(meta, slot)
        return pltpu.make_async_copy(
            dense.at[x0 + x, pl.ds(y0, BRICK)], dh_out.at[slot, x], sem_dh.at[slot, x]
        )

    for slot in range(SLOTS):

        @pl.when(slot < occupied)
        def _():
            def begin(x, carry):
                conv_copy(slot, x).start()
                og_copy(slot, x).start()
                return carry

            lax.fori_loop(0, BRICK, begin, 0)

    def clear(x, carry):
        for col in range(BRICK):
            blank[x, col] = jnp.zeros((CHANS, DEPTH), BF16)
        return carry

    lax.fori_loop(0, BRICK, clear, 0)

    def zero_copy(slot):
        x0, y0 = corner(meta, slot)
        return pltpu.make_async_copy(
            blank, normed_out.at[pl.ds(x0, BRICK), pl.ds(y0, BRICK)], sem_zero.at[slot]
        )

    for slot in range(4):

        @pl.when(slot >= occupied)
        def _():
            zero_copy(slot).start()

    zero_pillars(meta, dense, 0)

    total, square, upsum, cross = [totals[k : k + 1] for k in range(4)]
    count = jnp.sum(totals[4:5])
    gain, bias = params[0:1], params[1:2]
    mean = total / count
    inv_std = lax.rsqrt(square / count - mean * mean + EPSILON)
    gain_grad = inv_std * (cross - mean * upsum)
    sums_out[...] = jnp.zeros(sums_out.shape, F32)
    sums_out[0:1] = gain_grad
    sums_out[1:2] = upsum
    mean_c, inv_c, gain_c, bias_c = spread(mean), spread(inv_std), spread(gain), spread(bias)
    up_c, cross_c = spread(upsum / count), spread(gain_grad / count)
    scale_c = spread(gain * inv_std)

    for slot in range(SLOTS):

        @pl.when(slot < occupied)
        def _():
            x0, y0 = corner(meta, slot)

            def row(x, carry):
                conv_copy(slot, x).wait()
                og_copy(slot, x).wait()
                active = mask[x0 + x, pl.ds(y0, BRICK), :]
                for col in range(BRICK):
                    keep = active[col : col + 1]
                    normed = (convs[slot, x, col] - mean_c) * inv_c
                    ys[slot, x, col] = ((gain_c * normed + bias_c) * keep).astype(BF16)
                    up = grads[slot, x, col].astype(F32)
                    dense[x0 + x, y0 + col] = (
                        scale_c * (up - up_c - normed * cross_c) * keep
                    ).astype(BF16)
                y_copy(slot, x).start()
                dh_copy(slot, x).start()
                return carry

            lax.fori_loop(0, BRICK, row, 0)

    rims = [
        pltpu.make_async_copy(dense.at[0], x_low, sem_rim.at[0]),
        pltpu.make_async_copy(dense.at[15], x_high, sem_rim.at[1]),
        pltpu.make_async_copy(dense.at[:, 0], y_low, sem_rim.at[2]),
        pltpu.make_async_copy(dense.at[:, 15], y_high, sem_rim.at[3]),
    ]
    for copy in rims:
        copy.start()
    for copy in rims:
        copy.wait()
    for slot in range(4):

        @pl.when(slot >= occupied)
        def _():
            zero_copy(slot).wait()

    for slot in range(SLOTS):

        @pl.when(slot < occupied)
        def _():
            def drain(x, carry):
                y_copy(slot, x).wait()
                dh_copy(slot, x).wait()
                return carry

            lax.fori_loop(0, BRICK, drain, 0)


def normalize(meta, totals, params, conv, out_grad, mask):
    block = (SLOTS, BRICK, BRICK, CHANS, DEPTH)
    rim = jax.ShapeDtypeStruct((16, CHANS, DEPTH), BF16)
    return pl.pallas_call(
        norm_kernel,
        name="normalize",
        out_shape=(
            jax.ShapeDtypeStruct((16, 16, CHANS, DEPTH), BF16),
            jax.ShapeDtypeStruct(block, BF16),
            rim,
            rim,
            rim,
            rim,
            jax.ShapeDtypeStruct((8, DEPTH), F32),
        ),
        in_specs=[SMEM, VMEM, VMEM, ANY, ANY, VMEM],
        out_specs=(ANY, ANY, ANY, ANY, ANY, ANY, VMEM),
        scratch_shapes=[
            pltpu.VMEM(block, F32),
            pltpu.VMEM(block, BF16),
            pltpu.VMEM(block, BF16),
            pltpu.VMEM((16, 16, CHANS, DEPTH), BF16),
            pltpu.VMEM((BRICK, BRICK, CHANS, DEPTH), BF16),
            pltpu.SemaphoreType.DMA((SLOTS, BRICK)),
            pltpu.SemaphoreType.DMA((SLOTS, BRICK)),
            pltpu.SemaphoreType.DMA((SLOTS, BRICK)),
            pltpu.SemaphoreType.DMA((SLOTS, BRICK)),
            pltpu.SemaphoreType.DMA((4,)),
            pltpu.SemaphoreType.DMA((4,)),
        ],
        compiler_params=pltpu.CompilerParams(vmem_limit_bytes=VMEM_LIMIT),
        cost_estimate=pl.CostEstimate(flops=30_000_000, bytes_accessed=20_000_000, transcendentals=0),
    )(meta, totals, params, conv, out_grad, mask)


def weight_kernel(
    meta, features, mask, xm, xp, ym, yp, dh, out, field, grads, acc, sem_rim, sem_in, sem_dh
):
    occupied = meta[8]
    rims = rim_copies((xm, xp, ym, yp), field, sem_rim)
    for copy in rims:
        copy.start()
    loads = []
    for slot in range(SLOTS):
        x0, y0 = corner(meta, slot)
        loads.append(
            (
                pltpu.make_async_copy(
                    features.at[pl.ds(x0, BRICK), pl.ds(y0, BRICK)],
                    field.at[pl.ds(x0 + 1, BRICK), pl.ds(y0 + 1, BRICK)],
                    sem_in.at[slot],
                ),
                pltpu.make_async_copy(dh.at[slot], grads.at[slot], sem_dh.at[slot]),
            )
        )
    for slot in range(SLOTS):

        @pl.when(slot < occupied)
        def _():
            loads[slot][0].start()
            loads[slot][1].start()

    zero_pillars(meta, field, 1)
    acc[...] = jnp.zeros(acc.shape, F32)
    for copy in rims:
        copy.wait()
    for slot in range(SLOTS):

        @pl.when(slot < occupied)
        def _():
            loads[slot][0].wait()
            mask_pillar(meta, slot, mask, field)

    lane = lax.broadcasted_iota(jnp.int32, (CHANS, DEPTH), 1)
    for slot in range(SLOTS):

        @pl.when(slot < occupied)
        def _():
            x0, y0 = corner(meta, slot)
            loads[slot][1].wait()

            def row(x, carry):
                shifted = [[], [], []]
                for col in range(BRICK):
                    here = grads[slot, x, col]
                    wide = here.astype(F32)
                    shifted[0].append(
                        jnp.where(lane == DEPTH - 1, 0.0, pltpu.roll(wide, DEPTH - 1, 1)).astype(BF16)
                    )
                    shifted[1].append(here)
                    shifted[2].append(
                        jnp.where(lane == 0, 0.0, pltpu.roll(wide, 1, 1)).astype(BF16)
                    )
                left = jnp.concatenate([jnp.concatenate(s, axis=1) for s in shifted], axis=0)
                right = []
                for a in range(3):
                    for b in range(3):
                        right.append(
                            jnp.concatenate(
                                [field[x0 + x + a, y0 + b + col] for col in range(BRICK)], axis=1
                            )
                        )
                right.append(jnp.zeros((COLS - 9 * CHANS, BRICK * DEPTH), BF16))
                acc[...] += lax.dot_general(
                    left,
                    jnp.concatenate(right, axis=0),
                    (((1,), (1,)), ((), ())),
                    preferred_element_type=F32,
                )
                return carry

            lax.fori_loop(0, BRICK, row, 0)

    for tile in range(TILES):
        out[ROWS * tile : ROWS * (tile + 1)] = acc[:, DEPTH * tile : DEPTH * (tile + 1)]
    out[ROWS * TILES :] = jnp.zeros((2048 - ROWS * TILES, DEPTH), F32)


def weight_terms(meta, features, mask, rims, dh):
    return pl.pallas_call(
        weight_kernel,
        name="weight_terms",
        out_shape=jax.ShapeDtypeStruct((2048, DEPTH), F32),
        in_specs=[SMEM, ANY, VMEM, ANY, ANY, ANY, ANY, ANY],
        out_specs=VMEM,
        scratch_shapes=[
            pltpu.VMEM((18, 18, CHANS, DEPTH), BF16),
            pltpu.VMEM((SLOTS, BRICK, BRICK, CHANS, DEPTH), BF16),
            pltpu.VMEM((ROWS, COLS), F32),
            pltpu.SemaphoreType.DMA((4,)),
            pltpu.SemaphoreType.DMA((SLOTS,)),
            pltpu.SemaphoreType.DMA((SLOTS,)),
        ],
        compiler_params=pltpu.CompilerParams(vmem_limit_bytes=VMEM_LIMIT),
        cost_estimate=pl.CostEstimate(flops=8_200_000_000, bytes_accessed=8_000_000, transcendentals=0),
    )(meta, features, mask, *rims, dh)


def backward_kernel(
    meta, dh, mask, xm, xp, ym, yp, kernel_ref, out, field, results, blank, sem_rim, sem_in, sem_out, sem_zero
):
    occupied = meta[8]
    rims = rim_copies((xm, xp, ym, yp), field, sem_rim)
    for copy in rims:
        copy.start()
    loads = []
    for slot in range(SLOTS):
        x0, y0 = corner(meta, slot)
        loads.append(
            pltpu.make_async_copy(
                dh.at[slot], field.at[pl.ds(x0 + 1, BRICK), pl.ds(y0 + 1, BRICK)], sem_in.at[slot]
            )
        )
    for slot in range(SLOTS):

        @pl.when(slot < occupied)
        def _():
            loads[slot].start()

    def clear(x, carry):
        for col in range(BRICK):
            blank[x, col] = jnp.zeros((CHANS, DEPTH), BF16)
        return carry

    lax.fori_loop(0, BRICK, clear, 0)

    def zero_copy(slot):
        x0, y0 = corner(meta, slot)
        return pltpu.make_async_copy(
            blank, out.at[pl.ds(x0, BRICK), pl.ds(y0, BRICK)], sem_zero.at[slot]
        )

    for slot in range(4):

        @pl.when(slot >= occupied)
        def _():
            zero_copy(slot).start()

    zero_pillars(meta, field, 1)
    for copy in rims:
        copy.wait()
    for slot in range(SLOTS):

        @pl.when(slot < occupied)
        def _():
            loads[slot].wait()

    def out_copy(slot, x):
        x0, y0 = corner(meta, slot)
        return pltpu.make_async_copy(
            results.at[slot, x], out.at[x0 + x, pl.ds(y0, BRICK)], sem_out.at[slot, x]
        )

    for slot in range(SLOTS):

        @pl.when(slot < occupied)
        def _():
            x0, y0 = corner(meta, slot)

            def row(x, carry):
                active = mask[x0 + x, pl.ds(y0, BRICK), :]
                outs = column_convs(field, kernel_ref, x0 + x, y0, True)
                for col in range(BRICK):
                    results[slot, x, col] = (outs[col] * active[col : col + 1]).astype(BF16)
                out_copy(slot, x).start()
                return carry

            lax.fori_loop(0, BRICK, row, 0)

    for slot in range(4):

        @pl.when(slot >= occupied)
        def _():
            zero_copy(slot).wait()

    for slot in range(SLOTS):

        @pl.when(slot < occupied)
        def _():
            def drain(x, carry):
                out_copy(slot, x).wait()
                return carry

            lax.fori_loop(0, BRICK, drain, 0)


def backward(meta, dh, mask, rims, kernel):
    return pl.pallas_call(
        backward_kernel,
        name="backward",
        out_shape=jax.ShapeDtypeStruct((16, 16, CHANS, DEPTH), BF16),
        in_specs=[SMEM, ANY, VMEM, ANY, ANY, ANY, ANY, VMEM],
        out_specs=ANY,
        scratch_shapes=[
            pltpu.VMEM((18, 18, CHANS, DEPTH), BF16),
            pltpu.VMEM((SLOTS, BRICK, BRICK, CHANS, DEPTH), BF16),
            pltpu.VMEM((BRICK, BRICK, CHANS, DEPTH), BF16),
            pltpu.SemaphoreType.DMA((4,)),
            pltpu.SemaphoreType.DMA((SLOTS,)),
            pltpu.SemaphoreType.DMA((SLOTS, BRICK)),
            pltpu.SemaphoreType.DMA((4,)),
        ],
        compiler_params=pltpu.CompilerParams(vmem_limit_bytes=VMEM_LIMIT),
        cost_estimate=pl.CostEstimate(flops=8_200_000_000, bytes_accessed=14_000_000, transcendentals=0),
    )(meta, dh, mask, *rims, kernel)


def exchange(x_low, x_high, y_low, y_high):
    slabs, subs = lax.axis_size("slab"), lax.axis_size("sub")
    ahead = [(i, i + 1) for i in range(slabs - 1)]
    behind = [(i + 1, i) for i in range(slabs - 1)]
    xm = lax.ppermute(x_high, "slab", ahead)
    xp = lax.ppermute(x_low, "slab", behind)
    ahead = [(i, i + 1) for i in range(subs - 1)]
    behind = [(i + 1, i) for i in range(subs - 1)]
    first, last = slice(0, 1), slice(15, 16)
    ym = lax.ppermute(jnp.concatenate([xm[last], y_high, xp[last]]), "sub", ahead)
    yp = lax.ppermute(jnp.concatenate([xm[first], y_low, xp[first]]), "sub", behind)
    return (xm, xp, ym, yp)


def all_sum(rows):
    spread_rows = jnp.broadcast_to(rows[None], (DEVICES,) + rows.shape)
    gathered = lax.all_to_all(spread_rows, ("slab", "sub"), 0, 0, tiled=True)
    return jnp.sum(gathered, axis=0)


def all_sum_big(terms):
    pieces = terms.reshape(DEVICES, 16, DEPTH)
    mine = jnp.sum(lax.all_to_all(pieces, ("slab", "sub"), 0, 0, tiled=True), axis=0)
    copies = jnp.broadcast_to(mine[None], pieces.shape)
    return lax.all_to_all(copies, ("slab", "sub"), 0, 0, tiled=True).reshape(terms.shape)


def tap_kernels(weight):
    taps = weight.reshape(3, 3, 3, CHANS, CHANS)
    ahead = taps.transpose(2, 3, 0, 1, 4).reshape(ROWS, 9 * CHANS)
    back = taps[::-1, ::-1].transpose(2, 4, 0, 1, 3).reshape(ROWS, 9 * CHANS)
    edge = ((0, 0), (0, COLS - 9 * CHANS))
    return jnp.pad(ahead, edge), jnp.pad(back, edge)


def body(features, voxel_mask, weight, norm_gain, norm_bias, out_grad):
    mask = voxel_mask.astype(F32)
    mask_bf = voxel_mask.astype(BF16)[:, :, None, :]
    meta = slot_table(voxel_mask)
    rims = exchange(
        features[0] * mask_bf[0],
        features[15] * mask_bf[15],
        features[:, 0] * mask_bf[:, 0],
        features[:, 15] * mask_bf[:, 15],
    )
    ahead, back = tap_kernels(weight)
    conv, stats = forward(meta, features, out_grad, mask, rims, ahead)
    totals = all_sum(stats)
    params = jnp.pad(jnp.stack([norm_gain, norm_bias]), ((0, 6), (0, DEPTH - CHANS)))
    normed_out, dh, x_low, x_high, y_low, y_high, sums = normalize(
        meta, totals, params, conv, out_grad, mask
    )
    grad_rims = exchange(x_low, x_high, y_low, y_high)
    terms = weight_terms(meta, features, mask, rims, dh)
    feature_grad = backward(meta, dh, mask, grad_rims, back)
    summed = all_sum_big(terms)
    flat = summed[: ROWS * TILES].reshape(TILES, 3, CHANS, DEPTH).transpose(1, 2, 0, 3)
    flat = flat.reshape(3, CHANS, COLS)[:, :, : 9 * CHANS].reshape(3, CHANS, 9, CHANS)
    weight_grad = flat.transpose(2, 0, 1, 3).reshape(27, CHANS, CHANS)
    return (normed_out, feature_grad, weight_grad, sums[0, :CHANS], sums[1, :CHANS])


def solution(mesh):
    placed = (
        P("slab", "sub", None, None),
        P("slab", "sub", None),
        P(),
        P(),
        P(),
        P("slab", "sub", None, None),
    )
    return jax.shard_map(
        body,
        mesh=mesh,
        in_specs=placed,
        out_specs=(P("slab", "sub", None, None), P("slab", "sub", None, None), P(), P(), P()),
        check_vma=False,
    )
```

```python
import functools

import jax
import jax.numpy as jnp
from jax import lax
from jax.experimental import pallas as pl
from jax.experimental.pallas import tpu as pltpu
from jax.sharding import PartitionSpec as P

BRICK = 8
SLOTS = 2
EPSILON = 1e-05
DEVICES = 128
CHANS = 96
DEPTH = 128
TILES = 7
ROWS = 3 * CHANS
COLS = TILES * DEPTH
F32 = jnp.float32
BF16 = jnp.bfloat16
FIELD = (18, 18, CHANS, DEPTH)
BLOCKS = (SLOTS, BRICK, BRICK, CHANS, DEPTH)
MIB = 1024 * 1024
WIDE_CONVS = (24,) + BLOCKS[1:]
WIDE_SLOPES = (48,) + BLOCKS[1:]

ANY = pl.BlockSpec(memory_space=pl.ANY)
VMEM = pl.BlockSpec(memory_space=pltpu.VMEM)
SMEM = pl.BlockSpec(memory_space=pltpu.SMEM)
HBM = pl.BlockSpec(memory_space=pltpu.HBM)


def params_of(mib, **more):
    return pltpu.CompilerParams(vmem_limit_bytes=mib * MIB, **more)


def cost(flops, moved):
    return pl.CostEstimate(flops=flops, bytes_accessed=moved, transcendentals=0)


def corner(meta, slot):
    return (pl.multiple_of(meta[2 * slot], BRICK), pl.multiple_of(meta[2 * slot + 1], BRICK))


def active_rows(mask, x, y0):
    return mask[x, pl.ds(y0, BRICK), :].astype(F32)


def each_row(occupied, step):
    for slot in range(SLOTS):

        @pl.when(slot < occupied)
        def _():
            lax.fori_loop(0, BRICK, lambda x, carry: (step(slot, x), carry)[1], 0)


def clear_pillars(meta, field):
    for slot in range(4):

        @pl.when(slot >= meta[8])
        def _():
            x0, y0 = corner(meta, slot)

            def clear(row, carry):
                for col in range(BRICK):
                    field[x0 + row + 1, y0 + col + 1] = jnp.zeros((CHANS, DEPTH), BF16)
                return carry

            lax.fori_loop(0, BRICK, clear, 0)


def fill_rims(field, rims, sems):
    xm, xp, ym, yp = rims
    copies = [
        pltpu.make_async_copy(xm, field.at[0, pl.ds(1, 16)], sems.at[0]),
        pltpu.make_async_copy(xp, field.at[17, pl.ds(1, 16)], sems.at[1]),
        pltpu.make_async_copy(ym, field.at[:, 0], sems.at[2]),
        pltpu.make_async_copy(yp, field.at[:, 17], sems.at[3]),
    ]
    for copy in copies:
        copy.start()
    return copies


def take_rims(field, rims, sems):
    inner = pl.ds(1, 16)
    copies = [
        pltpu.make_async_copy(field.at[1, inner], rims[0], sems.at[0]),
        pltpu.make_async_copy(field.at[16, inner], rims[1], sems.at[1]),
        pltpu.make_async_copy(field.at[inner, 1], rims[2].at[inner], sems.at[2]),
        pltpu.make_async_copy(field.at[inner, 16], rims[3].at[inner], sems.at[3]),
    ]
    for copy in copies:
        copy.start()
    for copy in copies:
        copy.wait()


RIM = jax.ShapeDtypeStruct((16, CHANS, DEPTH), BF16)
LONG = jax.ShapeDtypeStruct((18, CHANS, DEPTH), BF16)


def prepare_kernel(features, mask, x_low, x_high, y_low, y_high, meta, faces, sides, sem_in, sem_out):
    loads = [
        pltpu.make_async_copy(features.at[0], faces.at[0], sem_in.at[0]),
        pltpu.make_async_copy(features.at[15], faces.at[1], sem_in.at[1]),
        pltpu.make_async_copy(features.at[:, 0], sides.at[0], sem_in.at[2]),
        pltpu.make_async_copy(features.at[:, 15], sides.at[1], sem_in.at[3]),
    ]
    inner = pl.ds(1, 16)
    stores = [
        pltpu.make_async_copy(faces.at[0], x_low, sem_out.at[0]),
        pltpu.make_async_copy(faces.at[1], x_high, sem_out.at[1]),
        pltpu.make_async_copy(sides.at[0], y_low.at[inner], sem_out.at[2]),
        pltpu.make_async_copy(sides.at[1], y_high.at[inner], sem_out.at[3]),
    ]
    for load in loads:
        load.start()

    flags = []
    for px in range(2):
        for py in range(2):
            cells = mask[BRICK * px : BRICK * (px + 1), BRICK * py : BRICK * (py + 1), :]
            flags.append(jnp.max(cells))
    taken = jnp.int32(0)
    for flag in flags:
        taken = taken + flag
    meta[8] = taken
    full, free = jnp.int32(0), taken
    for place, flag in enumerate(flags):
        rank = jnp.where(flag == 1, full, free)
        meta[2 * rank] = jnp.int32(place // 2 * BRICK)
        meta[2 * rank + 1] = jnp.int32(place % 2 * BRICK)
        full = full + flag
        free = free + 1 - flag

    for which in range(2):
        loads[which].wait()
        for col in range(16):
            keep = jnp.broadcast_to(mask[15 * which, col : col + 1, :], (CHANS, DEPTH))
            faces[which, col] = faces[which, col] * keep.astype(F32).astype(BF16)
        stores[which].start()
    for which in range(2):
        loads[2 + which].wait()
        for row in range(16):
            keep = jnp.broadcast_to(mask[row, 15 * which : 15 * which + 1, :], (CHANS, DEPTH))
            sides[which, row] = sides[which, row] * keep.astype(F32).astype(BF16)
        stores[2 + which].start()
    for store in stores:
        store.wait()


def prepare(features, voxel_mask):
    return pl.pallas_call(
        prepare_kernel,
        name="prepare",
        out_shape=(RIM, RIM, LONG, LONG, jax.ShapeDtypeStruct((9,), jnp.int32)),
        in_specs=[HBM, VMEM],
        out_specs=(ANY, ANY, ANY, ANY, SMEM),
        scratch_shapes=[
            pltpu.VMEM((2, 16, CHANS, DEPTH), BF16),
            pltpu.VMEM((2, 16, CHANS, DEPTH), BF16),
            pltpu.SemaphoreType.DMA((4,)),
            pltpu.SemaphoreType.DMA((4,)),
        ],
        compiler_params=params_of(54),
        cost_estimate=cost(3_000_000, 3_000_000),
    )(features, voxel_mask)


def build_kernel(meta, features, mask, *refs):
    *rims, field, sem_rim = refs
    copies = fill_rims(field, rims, sem_rim) if rims else []

    def mask_row(slot, x):
        x0, y0 = corner(meta, slot)
        active = active_rows(mask, x0 + x, y0)
        for col in range(BRICK):
            keep = jnp.broadcast_to(active[col : col + 1], (CHANS, DEPTH)).astype(BF16)
            field[x0 + x + 1, y0 + col + 1] = features[x0 + x, y0 + col] * keep

    clear_pillars(meta, field)
    each_row(meta[8], mask_row)
    for copy in copies:
        copy.wait()


def build(meta, features, voxel_mask, rims=()):
    return pl.pallas_call(
        build_kernel,
        name="build_whole" if rims else "build",
        out_shape=jax.ShapeDtypeStruct(FIELD, BF16),
        in_specs=[SMEM, VMEM, VMEM] + [ANY] * len(rims),
        out_specs=VMEM,
        scratch_shapes=[pltpu.SemaphoreType.DMA((4,))],
        compiler_params=params_of(2),
        cost_estimate=cost(3_000_000, 6_000_000),
    )(meta, features, voxel_mask, *rims)


def column_convs(field, kernel_ref, x, y0, flipped):
    lane = lax.broadcasted_iota(jnp.int32, (CHANS, DEPTH), 1)
    up, down = (2, 0) if flipped else (0, 2)
    outs = []
    for pair in range(BRICK // 2):
        pieces = []
        for a in range(3):
            for b in range(3):
                col = y0 + 2 * pair + b
                pieces.append(jnp.concatenate([field[x + a, col], field[x + a, col + 1]], axis=1))
        pieces.append(jnp.zeros((COLS - 9 * CHANS, 2 * DEPTH), BF16))
        planes = jnp.dot(
            kernel_ref[...], jnp.concatenate(pieces, axis=0), preferred_element_type=F32
        )
        for half in range(2):
            part = [
                planes[CHANS * e : CHANS * (e + 1), DEPTH * half : DEPTH * (half + 1)]
                for e in range(3)
            ]
            outs.append(
                part[1]
                + jnp.where(lane == 0, 0.0, pltpu.roll(part[up], 1, 1))
                + jnp.where(lane == DEPTH - 1, 0.0, pltpu.roll(part[down], DEPTH - 1, 1))
            )
    return outs


def forward_kernel(
    meta, before, grads, mask, xm, xp, ym, yp, taps, field, conv_out, stats, convs, sums, sem_rim, sem_out
):
    def conv_copy(slot, x):
        return pltpu.make_async_copy(convs.at[slot, x], conv_out.at[slot, x], sem_out.at[slot, x])

    rims = fill_rims(field, (xm, xp, ym, yp), sem_rim)
    for copy in rims:
        copy.wait()
    sums[...] = jnp.zeros(sums.shape, F32)

    def row(slot, x):
        x0, y0 = corner(meta, slot)
        active = active_rows(mask, x0 + x, y0)
        outs = column_convs(field, taps, x0 + x, y0, False)
        total, square, upsum, cross = [sums[k] for k in range(4)]
        for col in range(BRICK):
            keep = active[col : col + 1]
            conv = outs[col] * keep
            convs[slot, x, col] = conv
            up = grads[x0 + x, y0 + col].astype(F32) * keep
            total = total + conv
            square = square + conv * conv
            upsum = upsum + up
            cross = cross + up * conv
        for k, value in enumerate((total, square, upsum, cross)):
            sums[k] = value
        sums[4, 0:BRICK] = sums[4, 0:BRICK] + active
        conv_copy(slot, x).start()

    each_row(meta[8], row)

    ones = jnp.ones((8, DEPTH), F32)
    rows = []
    for k in range(5):
        flat = lax.dot_general(
            ones,
            sums[k],
            (((1,), (1,)), ((), ())),
            precision=lax.Precision.HIGHEST,
            preferred_element_type=F32,
        )
        rows.append(flat[0:1])
    rows.append(jnp.zeros((3, CHANS), F32))
    packed = jnp.concatenate(
        [jnp.concatenate(rows, axis=0), jnp.zeros((8, DEPTH - CHANS), F32)], axis=1
    )
    stats[...] = jnp.broadcast_to(packed[None], stats.shape)
    each_row(meta[8], lambda slot, x: conv_copy(slot, x).wait())


def forward(meta, field, out_grad, voxel_mask, rims, taps):
    return pl.pallas_call(
        forward_kernel,
        name="forward",
        out_shape=(
            jax.ShapeDtypeStruct(FIELD, BF16),
            jax.ShapeDtypeStruct(WIDE_CONVS, F32),
            jax.ShapeDtypeStruct((DEVICES, 8, DEPTH), F32),
        ),
        in_specs=[SMEM, VMEM, VMEM, VMEM, ANY, ANY, ANY, ANY, VMEM],
        out_specs=(VMEM, HBM, VMEM),
        scratch_shapes=[
            pltpu.VMEM(BLOCKS, F32),
            pltpu.VMEM((5, CHANS, DEPTH), F32),
            pltpu.SemaphoreType.DMA((4,)),
            pltpu.SemaphoreType.DMA((SLOTS, BRICK)),
        ],
        input_output_aliases={1: 0},
        compiler_params=params_of(10),
        cost_estimate=cost(16_000_000_000, 4_000_000),
    )(meta, field, out_grad, voxel_mask, *rims, taps)[1:]


def spread(row):
    return jnp.transpose(jnp.broadcast_to(row, (DEPTH, DEPTH)))[0:CHANS]


def blank_kernel(meta, normed, feature, blank, sems):
    occupied = meta[8]

    def clear(x, carry):
        for col in range(BRICK):
            blank[x, col] = jnp.zeros((CHANS, DEPTH), BF16)
        return carry

    lax.fori_loop(0, BRICK, clear, 0)

    def copies(slot):
        x0, y0 = corner(meta, slot)
        spot = (pl.ds(x0, BRICK), pl.ds(y0, BRICK))
        return (
            pltpu.make_async_copy(blank, normed.at[spot], sems.at[slot, 0]),
            pltpu.make_async_copy(blank, feature.at[spot], sems.at[slot, 1]),
        )

    for slot in range(4):

        @pl.when(slot >= occupied)
        def _():
            for copy in copies(slot):
                copy.start()

    for slot in range(4):

        @pl.when(slot >= occupied)
        def _():
            for copy in copies(slot):
                copy.wait()


def blanks(meta):
    dense = jax.ShapeDtypeStruct((16, 16, CHANS, DEPTH), BF16)
    return pl.pallas_call(
        blank_kernel,
        name="blanks",
        out_shape=(dense, dense),
        in_specs=[SMEM],
        out_specs=(HBM, HBM),
        scratch_shapes=[
            pltpu.VMEM((BRICK, BRICK, CHANS, DEPTH), BF16),
            pltpu.SemaphoreType.DMA((4, 2)),
        ],
        compiler_params=params_of(3),
        cost_estimate=cost(1_000, 8_000_000),
    )(meta)


def norm_rows(totals):
    total, square, upsum, cross = [totals[k : k + 1] for k in range(4)]
    count = jnp.sum(totals[4:5])
    mean = total / count
    inv_std = lax.rsqrt(square / count - mean * mean + EPSILON)
    return count, mean, inv_std, upsum, cross


def slope_kernel(
    meta, gathered, params, conv, out_grad, mask, field, kept, x_low, x_high, y_low, y_high, sums_out, totals_out, convs, grads, sem_conv, sem_og, sem_kept, sem_rim
):
    occupied = meta[8]

    def loads(slot, x):
        x0, y0 = corner(meta, slot)
        return (
            pltpu.make_async_copy(conv.at[slot, x], convs.at[slot, x], sem_conv.at[slot, x]),
            pltpu.make_async_copy(
                out_grad.at[x0 + x, pl.ds(y0, BRICK)], grads.at[slot, x], sem_og.at[slot, x]
            ),
        )

    def begin(slot, x):
        for copy in loads(slot, x):
            copy.start()

    each_row(occupied, begin)

    def keep_row(slot, x):
        x0, y0 = corner(meta, slot)
        return pltpu.make_async_copy(
            field.at[x0 + x + 1, pl.ds(y0 + 1, BRICK)], kept.at[slot, x], sem_kept.at[slot, x]
        )

    clear_pillars(meta, field)
    totals = jnp.sum(gathered[...], axis=0)
    totals_out[...] = totals
    count, mean, inv_std, upsum, cross = norm_rows(totals)
    gain_grad = inv_std * (cross - mean * upsum)
    sums_out[...] = jnp.zeros(sums_out.shape, F32)
    sums_out[0:1] = gain_grad
    sums_out[1:2] = upsum
    mean_c, inv_c = spread(mean), spread(inv_std)
    up_c, cross_c = spread(upsum / count), spread(gain_grad / count)
    scale_c = spread(params[0:1] * inv_std)

    def row(slot, x):
        x0, y0 = corner(meta, slot)
        for copy in loads(slot, x):
            copy.wait()
        active = active_rows(mask, x0 + x, y0)
        for col in range(BRICK):
            keep = active[col : col + 1]
            normed = (convs[slot, x, col] - mean_c) * inv_c
            up = grads[slot, x, col].astype(F32)
            field[x0 + x + 1, y0 + col + 1] = (
                scale_c * (up - up_c - normed * cross_c) * keep
            ).astype(BF16)
        keep_row(slot, x).start()

    each_row(occupied, row)
    take_rims(field, (x_low, x_high, y_low, y_high), sem_rim)
    each_row(occupied, lambda slot, x: keep_row(slot, x).wait())


def slopes(meta, gathered, params, conv, out_grad, voxel_mask):
    small = jax.ShapeDtypeStruct((8, DEPTH), F32)
    kept = jax.ShapeDtypeStruct(WIDE_SLOPES, BF16)
    return pl.pallas_call(
        slope_kernel,
        name="slopes",
        out_shape=(jax.ShapeDtypeStruct(FIELD, BF16), kept, RIM, RIM, LONG, LONG, small, small),
        in_specs=[SMEM, VMEM, VMEM, HBM, HBM, VMEM],
        out_specs=(VMEM, HBM, ANY, ANY, ANY, ANY, VMEM, VMEM),
        scratch_shapes=[
            pltpu.VMEM(BLOCKS, F32),
            pltpu.VMEM(BLOCKS, BF16),
            pltpu.SemaphoreType.DMA((SLOTS, BRICK)),
            pltpu.SemaphoreType.DMA((SLOTS, BRICK)),
            pltpu.SemaphoreType.DMA((SLOTS, BRICK)),
            pltpu.SemaphoreType.DMA((4,)),
        ],
        compiler_params=params_of(46),
        cost_estimate=cost(30_000_000, 12_000_000),
    )(meta, gathered, params, conv, out_grad, voxel_mask)


def normed_kernel(meta, totals, params, conv, mask, base, out, convs, ys, sem_conv, sems):
    def load(slot, x):
        return pltpu.make_async_copy(conv.at[slot, x], convs.at[slot, x], sem_conv.at[slot, x])

    each_row(meta[8], lambda slot, x: load(slot, x).start())
    _, mean, inv_std, _, _ = norm_rows(totals)
    mean_c, inv_c = spread(mean), spread(inv_std)
    gain_c, bias_c = spread(params[0:1]), spread(params[1:2])

    def copy(slot, x):
        x0, y0 = corner(meta, slot)
        return pltpu.make_async_copy(
            ys.at[slot, x], out.at[x0 + x, pl.ds(y0, BRICK)], sems.at[slot, x]
        )

    def row(slot, x):
        x0, y0 = corner(meta, slot)
        active = active_rows(mask, x0 + x, y0)
        load(slot, x).wait()
        for col in range(BRICK):
            normed = (convs[slot, x, col] - mean_c) * inv_c
            ys[slot, x, col] = ((gain_c * normed + bias_c) * active[col : col + 1]).astype(BF16)
        copy(slot, x).start()

    each_row(meta[8], row)
    each_row(meta[8], lambda slot, x: copy(slot, x).wait())


def normed_values(meta, totals, params, convs, voxel_mask, base):
    return pl.pallas_call(
        normed_kernel,
        name="normed_values",
        out_shape=jax.ShapeDtypeStruct((16, 16, CHANS, DEPTH), BF16),
        in_specs=[SMEM, VMEM, VMEM, HBM, VMEM, HBM],
        out_specs=HBM,
        scratch_shapes=[
            pltpu.VMEM(BLOCKS, F32),
            pltpu.VMEM(BLOCKS, BF16),
            pltpu.SemaphoreType.DMA((SLOTS, BRICK)),
            pltpu.SemaphoreType.DMA((SLOTS, BRICK)),
        ],
        input_output_aliases={5: 0},
        compiler_params=params_of(12),
        cost_estimate=cost(30_000_000, 8_000_000),
    )(meta, totals, params, convs, voxel_mask, base)


def weight_kernel(meta, field, slope, out, acc):
    acc[...] = jnp.zeros(acc.shape, F32)
    lane = lax.broadcasted_iota(jnp.int32, (CHANS, DEPTH), 1)

    def row(slot, x):
        x0, y0 = corner(meta, slot)
        shifted = [[], [], []]
        for col in range(BRICK):
            here = slope[x0 + x + 1, y0 + col + 1]
            wide = here.astype(F32)
            shifted[0].append(
                jnp.where(lane == DEPTH - 1, 0.0, pltpu.roll(wide, DEPTH - 1, 1)).astype(BF16)
            )
            shifted[1].append(here)
            shifted[2].append(jnp.where(lane == 0, 0.0, pltpu.roll(wide, 1, 1)).astype(BF16))
        left = jnp.concatenate([jnp.concatenate(s, axis=1) for s in shifted], axis=0)
        right = []
        for a in range(3):
            for b in range(3):
                cols = [field[x0 + x + a, y0 + b + col] for col in range(BRICK)]
                right.append(jnp.concatenate(cols, axis=1))
        right.append(jnp.zeros((COLS - 9 * CHANS, BRICK * DEPTH), BF16))
        acc[...] += lax.dot_general(
            left,
            jnp.concatenate(right, axis=0),
            (((1,), (1,)), ((), ())),
            preferred_element_type=F32,
        )

    each_row(meta[8], row)
    for tile in range(TILES):
        out[ROWS * tile : ROWS * (tile + 1)] = acc[:, DEPTH * tile : DEPTH * (tile + 1)]
    out[ROWS * TILES :] = jnp.zeros((2048 - ROWS * TILES, DEPTH), F32)


def weight_terms(meta, field, slope):
    return pl.pallas_call(
        weight_kernel,
        name="weight_terms",
        out_shape=jax.ShapeDtypeStruct((2048, DEPTH), F32),
        in_specs=[SMEM, VMEM, VMEM],
        out_specs=VMEM,
        scratch_shapes=[pltpu.VMEM((ROWS, COLS), F32)],
        compiler_params=params_of(4),
        cost_estimate=cost(16_000_000_000, 2_000_000),
    )(meta, field, slope)


def share_kernel(parts, out):
    mine = jnp.sum(parts[...], axis=0).astype(BF16)
    out[...] = jnp.broadcast_to(mine[None], out.shape)


def share(parts):
    return pl.pallas_call(
        share_kernel,
        name="share",
        out_shape=jax.ShapeDtypeStruct((DEVICES, 16, DEPTH), BF16),
        in_specs=[VMEM],
        out_specs=VMEM,
        compiler_params=params_of(2),
        cost_estimate=cost(300_000, 1_500_000),
    )(parts)


def arrange_kernel(flat, out):
    tiles = [flat[ROWS * t : ROWS * (t + 1)].astype(F32) for t in range(TILES)]
    for plane in range(9):
        tile, shift = CHANS * plane // DEPTH, CHANS * plane % DEPTH
        both = jnp.concatenate([tiles[tile], tiles[min(tile + 1, TILES - 1)]], axis=1)
        if shift:
            both = pltpu.roll(both, 2 * DEPTH - shift, 1)
        for e in range(3):
            out[3 * plane + e] = both[CHANS * e : CHANS * (e + 1), 0:CHANS]


def arrange(flat):
    return pl.pallas_call(
        arrange_kernel,
        name="arrange",
        out_shape=jax.ShapeDtypeStruct((27, CHANS, CHANS), F32),
        in_specs=[VMEM],
        out_specs=VMEM,
        compiler_params=params_of(4),
        cost_estimate=cost(300_000, 1_500_000),
    )(flat)


def backward_kernel(
    meta, kept, mask, xm, xp, ym, yp, taps, base, out, field, results, sem_rim, sem_in, sem_out
):
    occupied = meta[8]
    for slot in range(4):
        x0, y0 = corner(meta, slot)

        if slot < SLOTS:

            @pl.when(slot < occupied)
            def _():
                pltpu.make_async_copy(
                    kept.at[slot],
                    field.at[pl.ds(x0 + 1, BRICK), pl.ds(y0 + 1, BRICK)],
                    sem_in.at[slot],
                ).start()

    rims = fill_rims(field, (xm, xp, ym, yp), sem_rim)
    clear_pillars(meta, field)
    for copy in rims:
        copy.wait()
    for slot in range(SLOTS):
        x0, y0 = corner(meta, slot)

        @pl.when(slot < occupied)
        def _():
            pltpu.make_async_copy(
                kept.at[slot],
                field.at[pl.ds(x0 + 1, BRICK), pl.ds(y0 + 1, BRICK)],
                sem_in.at[slot],
            ).wait()

    def copy(slot, x):
        x0, y0 = corner(meta, slot)
        return pltpu.make_async_copy(
            results.at[slot, x], out.at[x0 + x, pl.ds(y0, BRICK)], sem_out.at[slot, x]
        )

    def row(slot, x):
        x0, y0 = corner(meta, slot)
        active = active_rows(mask, x0 + x, y0)
        outs = column_convs(field, taps, x0 + x, y0, True)
        for col in range(BRICK):
            results[slot, x, col] = (outs[col] * active[col : col + 1]).astype(BF16)
        copy(slot, x).start()

    each_row(occupied, row)
    each_row(occupied, lambda slot, x: copy(slot, x).wait())


def backward(meta, kept, voxel_mask, rims, taps, base):
    return pl.pallas_call(
        backward_kernel,
        name="backward",
        out_shape=jax.ShapeDtypeStruct((16, 16, CHANS, DEPTH), BF16),
        in_specs=[SMEM, HBM, VMEM, ANY, ANY, ANY, ANY, VMEM, HBM],
        out_specs=HBM,
        scratch_shapes=[
            pltpu.VMEM(FIELD, BF16),
            pltpu.VMEM(BLOCKS, BF16),
            pltpu.SemaphoreType.DMA((4,)),
            pltpu.SemaphoreType.DMA((SLOTS,)),
            pltpu.SemaphoreType.DMA((SLOTS, BRICK)),
        ],
        input_output_aliases={8: 0},
        compiler_params=params_of(15),
        cost_estimate=cost(16_000_000_000, 5_000_000),
    )(meta, kept, voxel_mask, *rims, taps, base)


def stitch_kernel(high, low, xm, xp, upper, lower, sems):
    copies = [
        pltpu.make_async_copy(xm.at[15], upper.at[0], sems.at[0]),
        pltpu.make_async_copy(xp.at[15], upper.at[17], sems.at[1]),
        pltpu.make_async_copy(xm.at[0], lower.at[0], sems.at[2]),
        pltpu.make_async_copy(xp.at[0], lower.at[17], sems.at[3]),
    ]
    for copy in copies:
        copy.start()
    for copy in copies:
        copy.wait()


def stitch(high, low, xm, xp):
    return pl.pallas_call(
        stitch_kernel,
        name="stitch",
        out_shape=(LONG, LONG),
        in_specs=[ANY, ANY, ANY, ANY],
        out_specs=(ANY, ANY),
        scratch_shapes=[pltpu.SemaphoreType.DMA((4,))],
        input_output_aliases={0: 0, 1: 1},
        compiler_params=params_of(1),
        cost_estimate=cost(1_000, 200_000),
    )(high, low, xm, xp)


def taps_kernel(weight, ahead, back):
    lane = lax.broadcasted_iota(jnp.int32, (CHANS, DEPTH), 1)
    side = jnp.zeros((CHANS, DEPTH - CHANS), F32)
    wide = [jnp.concatenate([weight[t].astype(F32), side], axis=1) for t in range(27)]
    below = jnp.zeros((DEPTH - CHANS, DEPTH), F32)

    def pack(blocks):
        tiles = []
        for tile in range(TILES):
            value = jnp.zeros((CHANS, DEPTH), F32)
            for place, block in enumerate(blocks):
                start = CHANS * place - DEPTH * tile
                if start >= DEPTH or start + CHANS <= 0:
                    continue
                moved = pltpu.roll(block, start % DEPTH, 1) if start % DEPTH else block
                here = jnp.logical_and(lane >= start, lane < start + CHANS)
                value = jnp.where(here, moved, value)
            tiles.append(value)
        return jnp.concatenate(tiles, axis=1).astype(BF16)

    for e in range(3):
        rows = slice(CHANS * e, CHANS * (e + 1))
        ahead[rows] = pack([wide[3 * plane + e] for plane in range(9)])
        turned = [
            jnp.transpose(jnp.concatenate([wide[3 * plane + e], below], axis=0))[0:CHANS]
            for plane in reversed(range(9))
        ]
        back[rows] = pack(turned)


def tap_kernels(weight):
    packed = jax.ShapeDtypeStruct((ROWS, COLS), BF16)
    return pl.pallas_call(
        taps_kernel,
        name="tap_kernels",
        out_shape=(packed, packed),
        in_specs=[VMEM],
        out_specs=(VMEM, VMEM),
        compiler_params=params_of(6),
        cost_estimate=cost(1_000_000, 2_000_000),
    )(weight)


def exchange_slabs(x_low, x_high):
    slabs = lax.axis_size("slab")
    xm = lax.ppermute(x_high, "slab", [(i, i + 1) for i in range(slabs - 1)])
    xp = lax.ppermute(x_low, "slab", [(i + 1, i) for i in range(slabs - 1)])
    return xm, xp


def exchange_subs(xm, xp, y_low, y_high):
    subs = lax.axis_size("sub")
    upper, lower = stitch(y_high, y_low, xm, xp)
    ym = lax.ppermute(upper, "sub", [(i, i + 1) for i in range(subs - 1)])
    yp = lax.ppermute(lower, "sub", [(i + 1, i) for i in range(subs - 1)])
    return ym, yp


def swap_all(pieces):
    return lax.all_to_all(pieces, ("slab", "sub"), 0, 0, tiled=True)


def body(features, voxel_mask, weight, norm_gain, norm_bias, out_grad):
    x_low, x_high, y_low, y_high, meta = prepare(features, voxel_mask)
    xm, xp = exchange_slabs(x_low, x_high)
    ym, yp = exchange_subs(xm, xp, y_low, y_high)
    rims = (xm, xp, ym, yp)
    field = build(meta, features, voxel_mask)
    ahead, back = tap_kernels(weight)
    params = jnp.pad(jnp.stack([norm_gain, norm_bias]), ((0, 6), (0, DEPTH - CHANS)))
    normed_base, feature_base = blanks(meta)
    field, normed_base, feature_base, params, back = lax.optimization_barrier(
        (field, normed_base, feature_base, params, back)
    )
    conv, stats = forward(meta, field, out_grad, voxel_mask, rims, ahead)
    slope, kept, x_low, x_high, y_low, y_high, sums, totals = slopes(
        meta, swap_all(stats), params, conv, out_grad, voxel_mask
    )
    xm, xp = exchange_slabs(x_low, x_high)
    rims, x_low = lax.optimization_barrier((rims, x_low))
    field = build(meta, features, voxel_mask, rims)
    xm, xp, slope, field = lax.optimization_barrier((xm, xp, slope, field))
    ym, yp = exchange_subs(xm, xp, y_low, y_high)
    terms = weight_terms(meta, field, slope)
    parts = swap_all(terms.reshape(DEVICES, 16, DEPTH))
    normed_out = normed_values(meta, totals, params, conv, voxel_mask, normed_base)
    shared = swap_all(share(parts))
    feature_grad = backward(meta, kept, voxel_mask, (xm, xp, ym, yp), back, feature_base)
    weight_grad = arrange(shared.reshape(2048, DEPTH))
    return (normed_out, feature_grad, weight_grad, sums[0, :CHANS], sums[1, :CHANS])


def solution(mesh):
    placed = (
        P("slab", "sub", None, None),
        P("slab", "sub", None),
        P(),
        P(),
        P(),
        P("slab", "sub", None, None),
    )
    return jax.shard_map(
        body,
        mesh=mesh,
        in_specs=placed,
        out_specs=(P("slab", "sub", None, None), P("slab", "sub", None, None), P(), P(), P()),
        check_vma=False,
    )
```

```python
import functools

import jax
import jax.numpy as jnp
from jax import lax
from jax.experimental import pallas as pl
from jax.experimental.pallas import tpu as pltpu
from jax.sharding import PartitionSpec as P

BRICK = 8
SLOTS = 2
EPSILON = 1e-05
DEVICES = 128
CHANS = 96
DEPTH = 128
TILES = 7
ROWS = 3 * CHANS
COLS = TILES * DEPTH
F32 = jnp.float32
BF16 = jnp.bfloat16
FIELD = (18, 18, CHANS, DEPTH)
BLOCKS = (SLOTS, BRICK, BRICK, CHANS, DEPTH)
MIB = 1024 * 1024
WIDE_CONVS = (24,) + BLOCKS[1:]
WIDE_SLOPES = (48,) + BLOCKS[1:]

ANY = pl.BlockSpec(memory_space=pl.ANY)
VMEM = pl.BlockSpec(memory_space=pltpu.VMEM)
SMEM = pl.BlockSpec(memory_space=pltpu.SMEM)
HBM = pl.BlockSpec(memory_space=pltpu.HBM)


def params_of(mib, **more):
    return pltpu.CompilerParams(vmem_limit_bytes=mib * MIB, **more)


def cost(flops, moved):
    return pl.CostEstimate(flops=flops, bytes_accessed=moved, transcendentals=0)


def corner(meta, slot):
    return (pl.multiple_of(meta[2 * slot], BRICK), pl.multiple_of(meta[2 * slot + 1], BRICK))


def active_rows(mask, x, y0):
    return mask[x, pl.ds(y0, BRICK), :].astype(F32)


def each_row(occupied, step):
    for slot in range(SLOTS):

        @pl.when(slot < occupied)
        def _():
            lax.fori_loop(0, BRICK, lambda x, carry: (step(slot, x), carry)[1], 0)


def clear_pillars(meta, field):
    for slot in range(4):

        @pl.when(slot >= meta[8])
        def _():
            x0, y0 = corner(meta, slot)

            def clear(row, carry):
                for col in range(BRICK):
                    field[x0 + row + 1, y0 + col + 1] = jnp.zeros((CHANS, DEPTH), BF16)
                return carry

            lax.fori_loop(0, BRICK, clear, 0)


def fill_rims(field, rims, sems):
    xm, xp, ym, yp = rims[:4]
    side = pl.ds(1, 16) if len(rims) > 4 else pl.ds(0, 18)
    copies = [
        pltpu.make_async_copy(xm, field.at[0, pl.ds(1, 16)], sems.at[0]),
        pltpu.make_async_copy(xp, field.at[17, pl.ds(1, 16)], sems.at[1]),
        pltpu.make_async_copy(ym, field.at[side, 0], sems.at[2]),
        pltpu.make_async_copy(yp, field.at[side, 17], sems.at[3]),
    ]
    for which, corners in enumerate(rims[4:]):
        for end in range(2):
            copies.append(
                pltpu.make_async_copy(
                    corners.at[end], field.at[17 * end, 17 * which], sems.at[4 + 2 * which + end]
                )
            )
    for copy in copies:
        copy.start()
    return copies


def take_rims(field, rims, sems):
    inner = pl.ds(1, 16)
    copies = [
        pltpu.make_async_copy(field.at[1, inner], rims[0], sems.at[0]),
        pltpu.make_async_copy(field.at[16, inner], rims[1], sems.at[1]),
        pltpu.make_async_copy(field.at[inner, 1], rims[2].at[inner], sems.at[2]),
        pltpu.make_async_copy(field.at[inner, 16], rims[3].at[inner], sems.at[3]),
    ]
    for copy in copies:
        copy.start()
    for copy in copies:
        copy.wait()


RIM = jax.ShapeDtypeStruct((16, CHANS, DEPTH), BF16)
LONG = jax.ShapeDtypeStruct((18, CHANS, DEPTH), BF16)


def prepare_kernel(features, mask, x_low, x_high, y_low, y_high, meta, sem_in):
    faces, sides = (x_low, x_high), (y_low, y_high)
    loads = [
        pltpu.make_async_copy(features.at[0], x_low, sem_in.at[0]),
        pltpu.make_async_copy(features.at[15], x_high, sem_in.at[1]),
        pltpu.make_async_copy(features.at[:, 0], y_low, sem_in.at[2]),
        pltpu.make_async_copy(features.at[:, 15], y_high, sem_in.at[3]),
    ]
    for load in loads:
        load.start()

    flags = []
    for px in range(2):
        for py in range(2):
            cells = mask[BRICK * px : BRICK * (px + 1), BRICK * py : BRICK * (py + 1), :]
            flags.append(jnp.max(cells))
    taken = jnp.int32(0)
    for flag in flags:
        taken = taken + flag
    meta[8] = taken
    full, free = jnp.int32(0), taken
    for place, flag in enumerate(flags):
        rank = jnp.where(flag == 1, full, free)
        meta[2 * rank] = jnp.int32(place // 2 * BRICK)
        meta[2 * rank + 1] = jnp.int32(place % 2 * BRICK)
        full = full + flag
        free = free + 1 - flag

    for which in range(2):
        loads[which].wait()
        for col in range(16):
            keep = jnp.broadcast_to(mask[15 * which, col : col + 1, :], (CHANS, DEPTH))
            faces[which][col] = faces[which][col] * keep.astype(F32).astype(BF16)
    for which in range(2):
        loads[2 + which].wait()
        for row in range(16):
            keep = jnp.broadcast_to(mask[row, 15 * which : 15 * which + 1, :], (CHANS, DEPTH))
            sides[which][row] = sides[which][row] * keep.astype(F32).astype(BF16)


def prepare(features, voxel_mask):
    return pl.pallas_call(
        prepare_kernel,
        name="prepare",
        out_shape=(RIM, RIM, RIM, RIM, jax.ShapeDtypeStruct((9,), jnp.int32)),
        in_specs=[HBM, VMEM],
        out_specs=(VMEM, VMEM, VMEM, VMEM, SMEM),
        scratch_shapes=[pltpu.SemaphoreType.DMA((4,))],
        compiler_params=params_of(54),
        cost_estimate=cost(3_000_000, 3_000_000),
    )(features, voxel_mask)


def build_kernel(meta, features, mask, *refs):
    *rims, field, sem_rim = refs
    copies = fill_rims(field, rims, sem_rim) if rims else []

    def mask_row(slot, x):
        x0, y0 = corner(meta, slot)
        active = active_rows(mask, x0 + x, y0)
        for col in range(BRICK):
            keep = jnp.broadcast_to(active[col : col + 1], (CHANS, DEPTH)).astype(BF16)
            field[x0 + x + 1, y0 + col + 1] = features[x0 + x, y0 + col] * keep

    clear_pillars(meta, field)
    each_row(meta[8], mask_row)
    for copy in copies:
        copy.wait()


def build(meta, features, voxel_mask, rims=()):
    return pl.pallas_call(
        build_kernel,
        name="build_whole" if rims else "build",
        out_shape=jax.ShapeDtypeStruct(FIELD, BF16),
        in_specs=[SMEM, VMEM, VMEM] + [ANY] * len(rims),
        out_specs=VMEM,
        scratch_shapes=[pltpu.SemaphoreType.DMA((8,))],
        compiler_params=params_of(2),
        cost_estimate=cost(3_000_000, 6_000_000),
    )(meta, features, voxel_mask, *rims)


def column_convs(field, kernel_ref, x, y0, flipped):
    lane = lax.broadcasted_iota(jnp.int32, (CHANS, DEPTH), 1)
    up, down = (2, 0) if flipped else (0, 2)
    outs = []
    for pair in range(BRICK // 2):
        pieces = []
        for a in range(3):
            for b in range(3):
                col = y0 + 2 * pair + b
                pieces.append(jnp.concatenate([field[x + a, col], field[x + a, col + 1]], axis=1))
        pieces.append(jnp.zeros((COLS - 9 * CHANS, 2 * DEPTH), BF16))
        planes = jnp.dot(
            kernel_ref[...], jnp.concatenate(pieces, axis=0), preferred_element_type=F32
        )
        for half in range(2):
            part = [
                planes[CHANS * e : CHANS * (e + 1), DEPTH * half : DEPTH * (half + 1)]
                for e in range(3)
            ]
            outs.append(
                part[1]
                + jnp.where(lane == 0, 0.0, pltpu.roll(part[up], 1, 1))
                + jnp.where(lane == DEPTH - 1, 0.0, pltpu.roll(part[down], DEPTH - 1, 1))
            )
    return outs


def forward_kernel(
    meta, before, grads, mask, xm, xp, ym, yp, cm, cp, taps, field, conv_out, stats, convs, sums, sem_rim, sem_out
):
    def conv_copy(slot, x):
        return pltpu.make_async_copy(convs.at[slot, x], conv_out.at[slot, x], sem_out.at[slot, x])

    rims = fill_rims(field, (xm, xp, ym, yp, cm, cp), sem_rim)
    for copy in rims:
        copy.wait()
    sums[...] = jnp.zeros(sums.shape, F32)

    def row(slot, x):
        x0, y0 = corner(meta, slot)
        active = active_rows(mask, x0 + x, y0)
        outs = column_convs(field, taps, x0 + x, y0, False)
        total, square, upsum, cross = [sums[k] for k in range(4)]
        for col in range(BRICK):
            keep = active[col : col + 1]
            conv = outs[col] * keep
            convs[slot, x, col] = conv
            up = grads[x0 + x, y0 + col].astype(F32) * keep
            total = total + conv
            square = square + conv * conv
            upsum = upsum + up
            cross = cross + up * conv
        for k, value in enumerate((total, square, upsum, cross)):
            sums[k] = value
        sums[4, 0:BRICK] = sums[4, 0:BRICK] + active
        conv_copy(slot, x).start()

    each_row(meta[8], row)

    ones = jnp.ones((8, DEPTH), F32)
    rows = []
    for k in range(5):
        flat = lax.dot_general(
            ones,
            sums[k],
            (((1,), (1,)), ((), ())),
            precision=lax.Precision.HIGHEST,
            preferred_element_type=F32,
        )
        rows.append(flat[0:1])
    rows.append(jnp.zeros((3, CHANS), F32))
    packed = jnp.concatenate(
        [jnp.concatenate(rows, axis=0), jnp.zeros((8, DEPTH - CHANS), F32)], axis=1
    )
    stats[...] = jnp.broadcast_to(packed[None], stats.shape)
    each_row(meta[8], lambda slot, x: conv_copy(slot, x).wait())


def forward(meta, field, out_grad, voxel_mask, rims, taps):
    return pl.pallas_call(
        forward_kernel,
        name="forward",
        out_shape=(
            jax.ShapeDtypeStruct(FIELD, BF16),
            jax.ShapeDtypeStruct(WIDE_CONVS, F32),
            jax.ShapeDtypeStruct((DEVICES, 8, DEPTH), F32),
        ),
        in_specs=[SMEM, VMEM, VMEM, VMEM] + [ANY] * 6 + [VMEM],
        out_specs=(VMEM, HBM, VMEM),
        scratch_shapes=[
            pltpu.VMEM(BLOCKS, F32),
            pltpu.VMEM((5, CHANS, DEPTH), F32),
            pltpu.SemaphoreType.DMA((8,)),
            pltpu.SemaphoreType.DMA((SLOTS, BRICK)),
        ],
        input_output_aliases={1: 0},
        compiler_params=params_of(10),
        cost_estimate=cost(16_000_000_000, 4_000_000),
    )(meta, field, out_grad, voxel_mask, *rims, taps)[1:]


def spread(row):
    return jnp.transpose(jnp.broadcast_to(row, (DEPTH, DEPTH)))[0:CHANS]


def blank_kernel(meta, normed, feature, blank, sems):
    occupied = meta[8]

    def clear(x, carry):
        for col in range(BRICK):
            blank[x, col] = jnp.zeros((CHANS, DEPTH), BF16)
        return carry

    lax.fori_loop(0, BRICK, clear, 0)

    def copies(slot):
        x0, y0 = corner(meta, slot)
        spot = (pl.ds(x0, BRICK), pl.ds(y0, BRICK))
        return (
            pltpu.make_async_copy(blank, normed.at[spot], sems.at[slot, 0]),
            pltpu.make_async_copy(blank, feature.at[spot], sems.at[slot, 1]),
        )

    for slot in range(4):

        @pl.when(slot >= occupied)
        def _():
            for copy in copies(slot):
                copy.start()

    for slot in range(4):

        @pl.when(slot >= occupied)
        def _():
            for copy in copies(slot):
                copy.wait()


def blanks(meta):
    dense = jax.ShapeDtypeStruct((16, 16, CHANS, DEPTH), BF16)
    return pl.pallas_call(
        blank_kernel,
        name="blanks",
        out_shape=(dense, dense),
        in_specs=[SMEM],
        out_specs=(HBM, HBM),
        scratch_shapes=[
            pltpu.VMEM((BRICK, BRICK, CHANS, DEPTH), BF16),
            pltpu.SemaphoreType.DMA((4, 2)),
        ],
        compiler_params=params_of(3),
        cost_estimate=cost(1_000, 8_000_000),
    )(meta)


def norm_rows(totals):
    total, square, upsum, cross = [totals[k : k + 1] for k in range(4)]
    count = jnp.sum(totals[4:5])
    mean = total / count
    inv_std = lax.rsqrt(square / count - mean * mean + EPSILON)
    return count, mean, inv_std, upsum, cross


def slope_kernel(
    meta, gathered, params, conv, grads, mask, field, kept, x_low, x_high, y_low, y_high, sums_out, totals_out, convs, sem_conv, sem_kept, sem_rim
):
    occupied = meta[8]

    def load(slot, x):
        return pltpu.make_async_copy(conv.at[slot, x], convs.at[slot, x], sem_conv.at[slot, x])

    each_row(occupied, lambda slot, x: load(slot, x).start())

    def keep_row(slot, x):
        x0, y0 = corner(meta, slot)
        return pltpu.make_async_copy(
            field.at[x0 + x + 1, pl.ds(y0 + 1, BRICK)], kept.at[slot, x], sem_kept.at[slot, x]
        )

    clear_pillars(meta, field)
    totals = jnp.sum(gathered[...], axis=0)
    totals_out[...] = totals
    count, mean, inv_std, upsum, cross = norm_rows(totals)
    gain_grad = inv_std * (cross - mean * upsum)
    sums_out[...] = jnp.zeros(sums_out.shape, F32)
    sums_out[0:1] = gain_grad
    sums_out[1:2] = upsum
    mean_c, inv_c = spread(mean), spread(inv_std)
    up_c, cross_c = spread(upsum / count), spread(gain_grad / count)
    scale_c = spread(params[0:1] * inv_std)

    def row(slot, x):
        x0, y0 = corner(meta, slot)
        load(slot, x).wait()
        active = active_rows(mask, x0 + x, y0)
        for col in range(BRICK):
            keep = active[col : col + 1]
            normed = (convs[slot, x, col] - mean_c) * inv_c
            up = grads[x0 + x, y0 + col].astype(F32)
            field[x0 + x + 1, y0 + col + 1] = (
                scale_c * (up - up_c - normed * cross_c) * keep
            ).astype(BF16)
        keep_row(slot, x).start()

    each_row(occupied, row)
    take_rims(field, (x_low, x_high, y_low, y_high), sem_rim)
    each_row(occupied, lambda slot, x: keep_row(slot, x).wait())


def slopes(meta, gathered, params, conv, out_grad, voxel_mask):
    small = jax.ShapeDtypeStruct((8, DEPTH), F32)
    kept = jax.ShapeDtypeStruct(WIDE_SLOPES, BF16)
    return pl.pallas_call(
        slope_kernel,
        name="slopes",
        out_shape=(jax.ShapeDtypeStruct(FIELD, BF16), kept, RIM, RIM, LONG, LONG, small, small),
        in_specs=[SMEM, VMEM, VMEM, HBM, VMEM, VMEM],
        out_specs=(VMEM, HBM, ANY, ANY, ANY, ANY, VMEM, VMEM),
        scratch_shapes=[
            pltpu.VMEM(BLOCKS, F32),
            pltpu.SemaphoreType.DMA((SLOTS, BRICK)),
            pltpu.SemaphoreType.DMA((SLOTS, BRICK)),
            pltpu.SemaphoreType.DMA((4,)),
        ],
        compiler_params=params_of(9),
        cost_estimate=cost(30_000_000, 12_000_000),
    )(meta, gathered, params, conv, out_grad, voxel_mask)


def normed_kernel(meta, totals, params, conv, mask, base, out, convs, ys, sem_conv, sems):
    def load(slot, x):
        return pltpu.make_async_copy(conv.at[slot, x], convs.at[slot, x], sem_conv.at[slot, x])

    each_row(meta[8], lambda slot, x: load(slot, x).start())
    _, mean, inv_std, _, _ = norm_rows(totals)
    mean_c, inv_c = spread(mean), spread(inv_std)
    gain_c, bias_c = spread(params[0:1]), spread(params[1:2])

    def copy(slot, x):
        x0, y0 = corner(meta, slot)
        return pltpu.make_async_copy(
            ys.at[slot, x], out.at[x0 + x, pl.ds(y0, BRICK)], sems.at[slot, x]
        )

    def row(slot, x):
        x0, y0 = corner(meta, slot)
        active = active_rows(mask, x0 + x, y0)
        load(slot, x).wait()
        for col in range(BRICK):
            normed = (convs[slot, x, col] - mean_c) * inv_c
            ys[slot, x, col] = ((gain_c * normed + bias_c) * active[col : col + 1]).astype(BF16)
        copy(slot, x).start()

    each_row(meta[8], row)
    each_row(meta[8], lambda slot, x: copy(slot, x).wait())


def normed_values(meta, totals, params, convs, voxel_mask, base):
    return pl.pallas_call(
        normed_kernel,
        name="normed_values",
        out_shape=jax.ShapeDtypeStruct((16, 16, CHANS, DEPTH), BF16),
        in_specs=[SMEM, VMEM, VMEM, HBM, VMEM, HBM],
        out_specs=HBM,
        scratch_shapes=[
            pltpu.VMEM(BLOCKS, F32),
            pltpu.VMEM(BLOCKS, BF16),
            pltpu.SemaphoreType.DMA((SLOTS, BRICK)),
            pltpu.SemaphoreType.DMA((SLOTS, BRICK)),
        ],
        input_output_aliases={5: 0},
        compiler_params=params_of(12),
        cost_estimate=cost(30_000_000, 8_000_000),
    )(meta, totals, params, convs, voxel_mask, base)


def weight_kernel(meta, field, slope, out, acc):
    acc[...] = jnp.zeros(acc.shape, F32)
    lane = lax.broadcasted_iota(jnp.int32, (CHANS, DEPTH), 1)

    def row(slot, x):
        x0, y0 = corner(meta, slot)
        shifted = [[], [], []]
        for col in range(BRICK):
            here = slope[x0 + x + 1, y0 + col + 1]
            wide = here.astype(F32)
            shifted[0].append(
                jnp.where(lane == DEPTH - 1, 0.0, pltpu.roll(wide, DEPTH - 1, 1)).astype(BF16)
            )
            shifted[1].append(here)
            shifted[2].append(jnp.where(lane == 0, 0.0, pltpu.roll(wide, 1, 1)).astype(BF16))
        left = jnp.concatenate([jnp.concatenate(s, axis=1) for s in shifted], axis=0)
        right = []
        for a in range(3):
            for b in range(3):
                cols = [field[x0 + x + a, y0 + b + col] for col in range(BRICK)]
                right.append(jnp.concatenate(cols, axis=1))
        right.append(jnp.zeros((COLS - 9 * CHANS, BRICK * DEPTH), BF16))
        acc[...] += lax.dot_general(
            left,
            jnp.concatenate(right, axis=0),
            (((1,), (1,)), ((), ())),
            preferred_element_type=F32,
        )

    each_row(meta[8], row)
    for tile in range(TILES):
        out[ROWS * tile : ROWS * (tile + 1)] = acc[:, DEPTH * tile : DEPTH * (tile + 1)]
    out[ROWS * TILES :] = jnp.zeros((2048 - ROWS * TILES, DEPTH), F32)


def weight_terms(meta, field, slope):
    return pl.pallas_call(
        weight_kernel,
        name="weight_terms",
        out_shape=jax.ShapeDtypeStruct((2048, DEPTH), F32),
        in_specs=[SMEM, VMEM, VMEM],
        out_specs=VMEM,
        scratch_shapes=[pltpu.VMEM((ROWS, COLS), F32)],
        compiler_params=params_of(4),
        cost_estimate=cost(16_000_000_000, 2_000_000),
    )(meta, field, slope)


def share_kernel(parts, out):
    mine = jnp.sum(parts[...], axis=0).astype(BF16)
    out[...] = jnp.broadcast_to(mine[None], out.shape)


def share(parts):
    return pl.pallas_call(
        share_kernel,
        name="share",
        out_shape=jax.ShapeDtypeStruct((DEVICES, 16, DEPTH), BF16),
        in_specs=[VMEM],
        out_specs=VMEM,
        compiler_params=params_of(2),
        cost_estimate=cost(300_000, 1_500_000),
    )(parts)


def arrange_kernel(flat, out):
    tiles = [flat[ROWS * t : ROWS * (t + 1)].astype(F32) for t in range(TILES)]
    for plane in range(9):
        tile, shift = CHANS * plane // DEPTH, CHANS * plane % DEPTH
        both = jnp.concatenate([tiles[tile], tiles[min(tile + 1, TILES - 1)]], axis=1)
        if shift:
            both = pltpu.roll(both, 2 * DEPTH - shift, 1)
        for e in range(3):
            out[3 * plane + e] = both[CHANS * e : CHANS * (e + 1), 0:CHANS]


def arrange(flat):
    return pl.pallas_call(
        arrange_kernel,
        name="arrange",
        out_shape=jax.ShapeDtypeStruct((27, CHANS, CHANS), F32),
        in_specs=[VMEM],
        out_specs=VMEM,
        compiler_params=params_of(4),
        cost_estimate=cost(300_000, 1_500_000),
    )(flat)


def backward_kernel(
    meta, kept, mask, xm, xp, ym, yp, taps, base, out, field, results, sem_rim, sem_in, sem_out
):
    occupied = meta[8]
    for slot in range(4):
        x0, y0 = corner(meta, slot)

        if slot < SLOTS:

            @pl.when(slot < occupied)
            def _():
                pltpu.make_async_copy(
                    kept.at[slot],
                    field.at[pl.ds(x0 + 1, BRICK), pl.ds(y0 + 1, BRICK)],
                    sem_in.at[slot],
                ).start()

    rims = fill_rims(field, (xm, xp, ym, yp), sem_rim)
    clear_pillars(meta, field)
    for copy in rims:
        copy.wait()
    for slot in range(SLOTS):
        x0, y0 = corner(meta, slot)

        @pl.when(slot < occupied)
        def _():
            pltpu.make_async_copy(
                kept.at[slot],
                field.at[pl.ds(x0 + 1, BRICK), pl.ds(y0 + 1, BRICK)],
                sem_in.at[slot],
            ).wait()

    def copy(slot, x):
        x0, y0 = corner(meta, slot)
        return pltpu.make_async_copy(
            results.at[slot, x], out.at[x0 + x, pl.ds(y0, BRICK)], sem_out.at[slot, x]
        )

    def row(slot, x):
        x0, y0 = corner(meta, slot)
        active = active_rows(mask, x0 + x, y0)
        outs = column_convs(field, taps, x0 + x, y0, True)
        for col in range(BRICK):
            results[slot, x, col] = (outs[col] * active[col : col + 1]).astype(BF16)
        copy(slot, x).start()

    each_row(occupied, row)
    each_row(occupied, lambda slot, x: copy(slot, x).wait())


def backward(meta, kept, voxel_mask, rims, taps, base):
    return pl.pallas_call(
        backward_kernel,
        name="backward",
        out_shape=jax.ShapeDtypeStruct((16, 16, CHANS, DEPTH), BF16),
        in_specs=[SMEM, HBM, VMEM, ANY, ANY, ANY, ANY, VMEM, HBM],
        out_specs=HBM,
        scratch_shapes=[
            pltpu.VMEM(FIELD, BF16),
            pltpu.VMEM(BLOCKS, BF16),
            pltpu.SemaphoreType.DMA((4,)),
            pltpu.SemaphoreType.DMA((SLOTS,)),
            pltpu.SemaphoreType.DMA((SLOTS, BRICK)),
        ],
        input_output_aliases={8: 0},
        compiler_params=params_of(15),
        cost_estimate=cost(16_000_000_000, 5_000_000),
    )(meta, kept, voxel_mask, *rims, taps, base)


def corner_kernel(xm, xp, upper, lower, sems):
    copies = [
        pltpu.make_async_copy(xm.at[15], upper.at[0], sems.at[0]),
        pltpu.make_async_copy(xp.at[15], upper.at[1], sems.at[1]),
        pltpu.make_async_copy(xm.at[0], lower.at[0], sems.at[2]),
        pltpu.make_async_copy(xp.at[0], lower.at[1], sems.at[3]),
    ]
    for copy in copies:
        copy.start()
    for copy in copies:
        copy.wait()


def corners_of(xm, xp):
    pair = jax.ShapeDtypeStruct((2, CHANS, DEPTH), BF16)
    return pl.pallas_call(
        corner_kernel,
        name="corners",
        out_shape=(pair, pair),
        in_specs=[ANY, ANY],
        out_specs=(ANY, ANY),
        scratch_shapes=[pltpu.SemaphoreType.DMA((4,))],
        compiler_params=params_of(1),
        cost_estimate=cost(1_000, 200_000),
    )(xm, xp)


def stitch_kernel(high, low, xm, xp, upper, lower, sems):
    copies = [
        pltpu.make_async_copy(xm.at[15], upper.at[0], sems.at[0]),
        pltpu.make_async_copy(xp.at[15], upper.at[17], sems.at[1]),
        pltpu.make_async_copy(xm.at[0], lower.at[0], sems.at[2]),
        pltpu.make_async_copy(xp.at[0], lower.at[17], sems.at[3]),
    ]
    for copy in copies:
        copy.start()
    for copy in copies:
        copy.wait()


def stitch(high, low, xm, xp):
    return pl.pallas_call(
        stitch_kernel,
        name="stitch",
        out_shape=(LONG, LONG),
        in_specs=[ANY, ANY, ANY, ANY],
        out_specs=(ANY, ANY),
        scratch_shapes=[pltpu.SemaphoreType.DMA((4,))],
        input_output_aliases={0: 0, 1: 1},
        compiler_params=params_of(1),
        cost_estimate=cost(1_000, 200_000),
    )(high, low, xm, xp)


def taps_kernel(weight, ahead, back):
    lane = lax.broadcasted_iota(jnp.int32, (CHANS, DEPTH), 1)
    side = jnp.zeros((CHANS, DEPTH - CHANS), F32)
    wide = [jnp.concatenate([weight[t].astype(F32), side], axis=1) for t in range(27)]
    below = jnp.zeros((DEPTH - CHANS, DEPTH), F32)

    def pack(blocks):
        tiles = []
        for tile in range(TILES):
            value = jnp.zeros((CHANS, DEPTH), F32)
            for place, block in enumerate(blocks):
                start = CHANS * place - DEPTH * tile
                if start >= DEPTH or start + CHANS <= 0:
                    continue
                moved = pltpu.roll(block, start % DEPTH, 1) if start % DEPTH else block
                here = jnp.logical_and(lane >= start, lane < start + CHANS)
                value = jnp.where(here, moved, value)
            tiles.append(value)
        return jnp.concatenate(tiles, axis=1).astype(BF16)

    for e in range(3):
        rows = slice(CHANS * e, CHANS * (e + 1))
        ahead[rows] = pack([wide[3 * plane + e] for plane in range(9)])
        turned = [
            jnp.transpose(jnp.concatenate([wide[3 * plane + e], below], axis=0))[0:CHANS]
            for plane in reversed(range(9))
        ]
        back[rows] = pack(turned)


def tap_kernels(weight):
    packed = jax.ShapeDtypeStruct((ROWS, COLS), BF16)
    return pl.pallas_call(
        taps_kernel,
        name="tap_kernels",
        out_shape=(packed, packed),
        in_specs=[VMEM],
        out_specs=(VMEM, VMEM),
        compiler_params=params_of(6),
        cost_estimate=cost(1_000_000, 2_000_000),
    )(weight)


def exchange_slabs(x_low, x_high):
    slabs = lax.axis_size("slab")
    xm = lax.ppermute(x_high, "slab", [(i, i + 1) for i in range(slabs - 1)])
    xp = lax.ppermute(x_low, "slab", [(i + 1, i) for i in range(slabs - 1)])
    return xm, xp


def exchange_subs(xm, xp, y_low, y_high):
    return shift_subs(*stitch(y_high, y_low, xm, xp))


def shift_subs(upper, lower):
    subs = lax.axis_size("sub")
    ym = lax.ppermute(upper, "sub", [(i, i + 1) for i in range(subs - 1)])
    yp = lax.ppermute(lower, "sub", [(i + 1, i) for i in range(subs - 1)])
    return ym, yp


def swap_all(pieces):
    return lax.all_to_all(pieces, ("slab", "sub"), 0, 0, tiled=True)


def body(features, voxel_mask, weight, norm_gain, norm_bias, out_grad):
    x_low, x_high, y_low, y_high, meta = prepare(features, voxel_mask)
    xm, xp = exchange_slabs(x_low, x_high)
    ym, yp = shift_subs(y_high, y_low)
    cm, cp = shift_subs(*corners_of(xm, xp))
    rims = (xm, xp, ym, yp, cm, cp)
    field = build(meta, features, voxel_mask)
    ahead, back = tap_kernels(weight)
    params = jnp.pad(jnp.stack([norm_gain, norm_bias]), ((0, 6), (0, DEPTH - CHANS)))
    field, params, back = lax.optimization_barrier((field, params, back))
    conv, stats = forward(meta, field, out_grad, voxel_mask, rims, ahead)
    slope, kept, x_low, x_high, y_low, y_high, sums, totals = slopes(
        meta, swap_all(stats), params, conv, out_grad, voxel_mask
    )
    xm, xp = exchange_slabs(x_low, x_high)
    rims, x_low = lax.optimization_barrier((rims, x_low))
    field = build(meta, features, voxel_mask, rims)
    xm, xp, slope, field = lax.optimization_barrier((xm, xp, slope, field))
    ym, yp = exchange_subs(xm, xp, y_low, y_high)
    terms = weight_terms(meta, field, slope)
    parts = swap_all(terms.reshape(DEVICES, 16, DEPTH))
    normed_base, feature_base = blanks(meta)
    normed_out = normed_values(meta, totals, params, conv, voxel_mask, normed_base)
    shared = swap_all(share(parts))
    feature_grad = backward(meta, kept, voxel_mask, (xm, xp, ym, yp), back, feature_base)
    weight_grad = arrange(shared.reshape(2048, DEPTH))
    return (normed_out, feature_grad, weight_grad, sums[0, :CHANS], sums[1, :CHANS])


def solution(mesh):
    placed = (
        P("slab", "sub", None, None),
        P("slab", "sub", None),
        P(),
        P(),
        P(),
        P("slab", "sub", None, None),
    )
    return jax.shard_map(
        body,
        mesh=mesh,
        in_specs=placed,
        out_specs=(P("slab", "sub", None, None), P("slab", "sub", None, None), P(), P(), P()),
        check_vma=False,
    )
```

```python
import functools

import jax
import jax.numpy as jnp
from jax import lax
from jax.experimental import pallas as pl
from jax.experimental.pallas import tpu as pltpu
from jax.sharding import PartitionSpec as P

BRICK = 8
SLOTS = 2
EPSILON = 1e-05
DEVICES = 128
CHANS = 96
DEPTH = 128
TILES = 7
ROWS = 3 * CHANS
COLS = TILES * DEPTH
F32 = jnp.float32
BF16 = jnp.bfloat16
FIELD = (18, 18, CHANS, DEPTH)
BLOCKS = (SLOTS, BRICK, BRICK, CHANS, DEPTH)
MIB = 1024 * 1024
WIDE_CONVS = (24,) + BLOCKS[1:]
WIDE_SLOPES = (48,) + BLOCKS[1:]

ANY = pl.BlockSpec(memory_space=pl.ANY)
VMEM = pl.BlockSpec(memory_space=pltpu.VMEM)
SMEM = pl.BlockSpec(memory_space=pltpu.SMEM)
HBM = pl.BlockSpec(memory_space=pltpu.HBM)


def params_of(mib, **more):
    return pltpu.CompilerParams(vmem_limit_bytes=mib * MIB, **more)


def cost(flops, moved):
    return pl.CostEstimate(flops=flops, bytes_accessed=moved, transcendentals=0)


def corner(meta, slot):
    return (pl.multiple_of(meta[2 * slot], BRICK), pl.multiple_of(meta[2 * slot + 1], BRICK))


def active_rows(mask, x, y0):
    return mask[x, pl.ds(y0, BRICK), :].astype(F32)


def each_row(occupied, step, unroll=1):
    for slot in range(SLOTS):

        @pl.when(slot < occupied)
        def _():
            lax.fori_loop(
                0, BRICK, lambda x, carry: (step(slot, x), carry)[1], 0, unroll=unroll
            )


def clear_pillars(meta, field):
    for slot in range(4):

        @pl.when(slot >= meta[8])
        def _():
            x0, y0 = corner(meta, slot)

            def clear(row, carry):
                for col in range(BRICK):
                    field[x0 + row + 1, y0 + col + 1] = jnp.zeros((CHANS, DEPTH), BF16)
                return carry

            lax.fori_loop(0, BRICK, clear, 0)


def near_ends(meta):
    return 1 - meta[9], 1 - meta[10]


def fill_rims(meta, field, rims, sems):
    x_end, y_end = near_ends(meta)
    side = pl.ds(1, 16) if len(rims) > 4 else pl.ds(0, 18)
    copies = []
    for turn in range(2):
        row = 17 * (x_end if turn == 0 else 1 - x_end)
        col = 17 * (y_end if turn == 0 else 1 - y_end)
        moves = [
            (rims[turn], field.at[row, pl.ds(1, 16)]),
            (rims[2 + turn], field.at[side, col]),
        ]
        if len(rims) > 4:
            moves += [(rims[4 + turn].at[end], field.at[17 * end, col]) for end in range(2)]
        for source, target in moves:
            copies.append(pltpu.make_async_copy(source, target, sems.at[len(copies)]))
    for copy in copies:
        copy.start()
    return copies


def take_rims(meta, field, rims, sems):
    x_end, y_end = near_ends(meta)
    inner = pl.ds(1, 16)
    copies = []
    for turn in range(2):
        row = 1 + 15 * (x_end if turn == 0 else 1 - x_end)
        col = 1 + 15 * (y_end if turn == 0 else 1 - y_end)
        copies += [
            pltpu.make_async_copy(field.at[row, inner], rims[turn], sems.at[turn]),
            pltpu.make_async_copy(
                field.at[inner, col], rims[2 + turn].at[inner], sems.at[2 + turn]
            ),
        ]
    for copy in copies:
        copy.start()
    for copy in copies:
        copy.wait()


RIM = jax.ShapeDtypeStruct((16, CHANS, DEPTH), BF16)
LONG = jax.ShapeDtypeStruct((18, CHANS, DEPTH), BF16)


def prepare_kernel(features, mask, x_even, x_odd, y_even, y_odd, meta, sem_in):
    faces, sides = (x_even, x_odd), (y_even, y_odd)
    meta[9] = lax.rem(lax.axis_index("slab"), 2)
    meta[10] = lax.rem(lax.axis_index("sub"), 2)
    x_end, y_end = near_ends(meta)
    rows, cols = (15 * x_end, 15 - 15 * x_end), (15 * y_end, 15 - 15 * y_end)
    loads = [
        pltpu.make_async_copy(features.at[rows[0]], x_even, sem_in.at[0]),
        pltpu.make_async_copy(features.at[rows[1]], x_odd, sem_in.at[1]),
        pltpu.make_async_copy(features.at[:, cols[0]], y_even, sem_in.at[2]),
        pltpu.make_async_copy(features.at[:, cols[1]], y_odd, sem_in.at[3]),
    ]
    for load in loads:
        load.start()

    flags = []
    for px in range(2):
        for py in range(2):
            cells = mask[BRICK * px : BRICK * (px + 1), BRICK * py : BRICK * (py + 1), :]
            flags.append(jnp.max(cells))
    taken = jnp.int32(0)
    for flag in flags:
        taken = taken + flag
    meta[8] = taken
    full, free = jnp.int32(0), taken
    for place, flag in enumerate(flags):
        rank = jnp.where(flag == 1, full, free)
        meta[2 * rank] = jnp.int32(place // 2 * BRICK)
        meta[2 * rank + 1] = jnp.int32(place % 2 * BRICK)
        full = full + flag
        free = free + 1 - flag

    for which in range(2):
        loads[which].wait()
        for col in range(16):
            keep = jnp.broadcast_to(mask[rows[which], col : col + 1, :], (CHANS, DEPTH))
            faces[which][col] = faces[which][col] * keep.astype(F32).astype(BF16)
    for which in range(2):
        loads[2 + which].wait()
        for row in range(16):
            keep = jnp.broadcast_to(mask[row, pl.ds(cols[which], 1), :], (CHANS, DEPTH))
            sides[which][row] = sides[which][row] * keep.astype(F32).astype(BF16)


def prepare(features, voxel_mask):
    return pl.pallas_call(
        prepare_kernel,
        name="prepare",
        out_shape=(RIM, RIM, RIM, RIM, jax.ShapeDtypeStruct((11,), jnp.int32)),
        in_specs=[HBM, VMEM],
        out_specs=(VMEM, VMEM, VMEM, VMEM, SMEM),
        scratch_shapes=[pltpu.SemaphoreType.DMA((4,))],
        compiler_params=params_of(54),
        cost_estimate=cost(3_000_000, 3_000_000),
    )(features, voxel_mask)


def build_kernel(meta, features, mask, *refs):
    *rims, field, sem_rim = refs
    copies = fill_rims(meta, field, rims, sem_rim) if rims else []

    def mask_row(slot, x):
        x0, y0 = corner(meta, slot)
        active = active_rows(mask, x0 + x, y0)
        for col in range(BRICK):
            keep = jnp.broadcast_to(active[col : col + 1], (CHANS, DEPTH)).astype(BF16)
            field[x0 + x + 1, y0 + col + 1] = features[x0 + x, y0 + col] * keep

    clear_pillars(meta, field)
    each_row(meta[8], mask_row)
    for copy in copies:
        copy.wait()


def build(meta, features, voxel_mask, rims=()):
    return pl.pallas_call(
        build_kernel,
        name="build_whole" if rims else "build",
        out_shape=jax.ShapeDtypeStruct(FIELD, BF16),
        in_specs=[SMEM, VMEM, VMEM] + [ANY] * len(rims),
        out_specs=VMEM,
        scratch_shapes=[pltpu.SemaphoreType.DMA((8,))],
        compiler_params=params_of(2),
        cost_estimate=cost(3_000_000, 6_000_000),
    )(meta, features, voxel_mask, *rims)


def column_convs(field, kernel_ref, x, y0, flipped):
    lane = lax.broadcasted_iota(jnp.int32, (CHANS, DEPTH), 1)
    up, down = (2, 0) if flipped else (0, 2)
    outs = []
    for pair in range(BRICK // 2):
        pieces = []
        for a in range(3):
            for b in range(3):
                col = y0 + 2 * pair + b
                pieces.append(jnp.concatenate([field[x + a, col], field[x + a, col + 1]], axis=1))
        pieces.append(jnp.zeros((COLS - 9 * CHANS, 2 * DEPTH), BF16))
        planes = jnp.dot(
            kernel_ref[...], jnp.concatenate(pieces, axis=0), preferred_element_type=F32
        )
        for half in range(2):
            part = [
                planes[CHANS * e : CHANS * (e + 1), DEPTH * half : DEPTH * (half + 1)]
                for e in range(3)
            ]
            outs.append(
                part[1]
                + jnp.where(lane == 0, 0.0, pltpu.roll(part[up], 1, 1))
                + jnp.where(lane == DEPTH - 1, 0.0, pltpu.roll(part[down], DEPTH - 1, 1))
            )
    return outs


def forward_kernel(
    meta, before, grads, mask, xm, xp, ym, yp, cm, cp, taps, field, conv_out, stats, convs, sums, sem_rim, sem_out
):
    def conv_copy(slot, x):
        return pltpu.make_async_copy(convs.at[slot, x], conv_out.at[slot, x], sem_out.at[slot, x])

    rims = fill_rims(meta, field, (xm, xp, ym, yp, cm, cp), sem_rim)
    for copy in rims:
        copy.wait()
    sums[...] = jnp.zeros(sums.shape, F32)

    def row(slot, x):
        x0, y0 = corner(meta, slot)
        active = active_rows(mask, x0 + x, y0)
        outs = column_convs(field, taps, x0 + x, y0, False)
        total, square, upsum, cross = [sums[k] for k in range(4)]
        for col in range(BRICK):
            keep = active[col : col + 1]
            conv = outs[col] * keep
            convs[slot, x, col] = conv
            up = grads[x0 + x, y0 + col].astype(F32) * keep
            total = total + conv
            square = square + conv * conv
            upsum = upsum + up
            cross = cross + up * conv
        for k, value in enumerate((total, square, upsum, cross)):
            sums[k] = value
        sums[4, 0:BRICK] = sums[4, 0:BRICK] + active
        conv_copy(slot, x).start()

    each_row(meta[8], row, unroll=2)

    ones = jnp.ones((8, DEPTH), F32)
    rows = []
    for k in range(5):
        flat = lax.dot_general(
            ones,
            sums[k],
            (((1,), (1,)), ((), ())),
            precision=lax.Precision.HIGHEST,
            preferred_element_type=F32,
        )
        rows.append(flat[0:1])
    rows.append(jnp.zeros((3, CHANS), F32))
    packed = jnp.concatenate(
        [jnp.concatenate(rows, axis=0), jnp.zeros((8, DEPTH - CHANS), F32)], axis=1
    )
    stats[...] = jnp.broadcast_to(packed[None], stats.shape)
    each_row(meta[8], lambda slot, x: conv_copy(slot, x).wait())


def forward(meta, field, out_grad, voxel_mask, rims, taps):
    return pl.pallas_call(
        forward_kernel,
        name="forward",
        out_shape=(
            jax.ShapeDtypeStruct(FIELD, BF16),
            jax.ShapeDtypeStruct(WIDE_CONVS, F32),
            jax.ShapeDtypeStruct((DEVICES, 8, DEPTH), F32),
        ),
        in_specs=[SMEM, VMEM, VMEM, VMEM] + [ANY] * 6 + [VMEM],
        out_specs=(VMEM, HBM, VMEM),
        scratch_shapes=[
            pltpu.VMEM(BLOCKS, F32),
            pltpu.VMEM((5, CHANS, DEPTH), F32),
            pltpu.SemaphoreType.DMA((8,)),
            pltpu.SemaphoreType.DMA((SLOTS, BRICK)),
        ],
        input_output_aliases={1: 0},
        compiler_params=params_of(10),
        cost_estimate=cost(16_000_000_000, 4_000_000),
    )(meta, field, out_grad, voxel_mask, *rims, taps)[1:]


def spread(row):
    return jnp.transpose(jnp.broadcast_to(row, (DEPTH, DEPTH)))[0:CHANS]


def blank_kernel(meta, normed, feature, blank, sems):
    occupied = meta[8]

    def clear(x, carry):
        for col in range(BRICK):
            blank[x, col] = jnp.zeros((CHANS, DEPTH), BF16)
        return carry

    lax.fori_loop(0, BRICK, clear, 0)

    def copies(slot):
        x0, y0 = corner(meta, slot)
        spot = (pl.ds(x0, BRICK), pl.ds(y0, BRICK))
        return (
            pltpu.make_async_copy(blank, normed.at[spot], sems.at[slot, 0]),
            pltpu.make_async_copy(blank, feature.at[spot], sems.at[slot, 1]),
        )

    for slot in range(4):

        @pl.when(slot >= occupied)
        def _():
            for copy in copies(slot):
                copy.start()

    for slot in range(4):

        @pl.when(slot >= occupied)
        def _():
            for copy in copies(slot):
                copy.wait()


def blanks(meta):
    dense = jax.ShapeDtypeStruct((16, 16, CHANS, DEPTH), BF16)
    return pl.pallas_call(
        blank_kernel,
        name="blanks",
        out_shape=(dense, dense),
        in_specs=[SMEM],
        out_specs=(HBM, HBM),
        scratch_shapes=[
            pltpu.VMEM((BRICK, BRICK, CHANS, DEPTH), BF16),
            pltpu.SemaphoreType.DMA((4, 2)),
        ],
        compiler_params=params_of(3),
        cost_estimate=cost(1_000, 8_000_000),
    )(meta)


def norm_rows(totals):
    total, square, upsum, cross = [totals[k : k + 1] for k in range(4)]
    count = jnp.sum(totals[4:5])
    mean = total / count
    inv_std = lax.rsqrt(square / count - mean * mean + EPSILON)
    return count, mean, inv_std, upsum, cross


def slope_kernel(
    meta, gathered, params, conv, grads, mask, field, kept, x_even, x_odd, y_even, y_odd, sums_out, totals_out, convs, sem_conv, sem_kept, sem_rim
):
    occupied = meta[8]

    def load(slot, x):
        return pltpu.make_async_copy(conv.at[slot, x], convs.at[slot, x], sem_conv.at[slot, x])

    each_row(occupied, lambda slot, x: load(slot, x).start())

    def keep_row(slot, x):
        x0, y0 = corner(meta, slot)
        return pltpu.make_async_copy(
            field.at[x0 + x + 1, pl.ds(y0 + 1, BRICK)], kept.at[slot, x], sem_kept.at[slot, x]
        )

    clear_pillars(meta, field)
    totals = jnp.sum(gathered[...], axis=0)
    totals_out[...] = totals
    count, mean, inv_std, upsum, cross = norm_rows(totals)
    gain_grad = inv_std * (cross - mean * upsum)
    sums_out[...] = jnp.zeros(sums_out.shape, F32)
    sums_out[0:1] = gain_grad
    sums_out[1:2] = upsum
    mean_c, inv_c = spread(mean), spread(inv_std)
    up_c, cross_c = spread(upsum / count), spread(gain_grad / count)
    scale_c = spread(params[0:1] * inv_std)

    def row(slot, x):
        x0, y0 = corner(meta, slot)
        load(slot, x).wait()
        active = active_rows(mask, x0 + x, y0)
        for col in range(BRICK):
            keep = active[col : col + 1]
            normed = (convs[slot, x, col] - mean_c) * inv_c
            up = grads[x0 + x, y0 + col].astype(F32)
            field[x0 + x + 1, y0 + col + 1] = (
                scale_c * (up - up_c - normed * cross_c) * keep
            ).astype(BF16)
        keep_row(slot, x).start()

    each_row(occupied, row)
    take_rims(meta, field, (x_even, x_odd, y_even, y_odd), sem_rim)
    each_row(occupied, lambda slot, x: keep_row(slot, x).wait())


def slopes(meta, gathered, params, conv, out_grad, voxel_mask):
    small = jax.ShapeDtypeStruct((8, DEPTH), F32)
    kept = jax.ShapeDtypeStruct(WIDE_SLOPES, BF16)
    return pl.pallas_call(
        slope_kernel,
        name="slopes",
        out_shape=(jax.ShapeDtypeStruct(FIELD, BF16), kept, RIM, RIM, LONG, LONG, small, small),
        in_specs=[SMEM, VMEM, VMEM, HBM, VMEM, VMEM],
        out_specs=(VMEM, HBM, ANY, ANY, ANY, ANY, VMEM, VMEM),
        scratch_shapes=[
            pltpu.VMEM(BLOCKS, F32),
            pltpu.SemaphoreType.DMA((SLOTS, BRICK)),
            pltpu.SemaphoreType.DMA((SLOTS, BRICK)),
            pltpu.SemaphoreType.DMA((4,)),
        ],
        compiler_params=params_of(9),
        cost_estimate=cost(30_000_000, 12_000_000),
    )(meta, gathered, params, conv, out_grad, voxel_mask)


def normed_kernel(meta, totals, params, conv, mask, base, out, convs, ys, sem_conv, sems):
    def load(slot, x):
        return pltpu.make_async_copy(conv.at[slot, x], convs.at[slot, x], sem_conv.at[slot, x])

    each_row(meta[8], lambda slot, x: load(slot, x).start())
    _, mean, inv_std, _, _ = norm_rows(totals)
    mean_c, inv_c = spread(mean), spread(inv_std)
    gain_c, bias_c = spread(params[0:1]), spread(params[1:2])

    def copy(slot, x):
        x0, y0 = corner(meta, slot)
        return pltpu.make_async_copy(
            ys.at[slot, x], out.at[x0 + x, pl.ds(y0, BRICK)], sems.at[slot, x]
        )

    def row(slot, x):
        x0, y0 = corner(meta, slot)
        active = active_rows(mask, x0 + x, y0)
        load(slot, x).wait()
        for col in range(BRICK):
            normed = (convs[slot, x, col] - mean_c) * inv_c
            ys[slot, x, col] = ((gain_c * normed + bias_c) * active[col : col + 1]).astype(BF16)
        copy(slot, x).start()

    each_row(meta[8], row)
    each_row(meta[8], lambda slot, x: copy(slot, x).wait())


def normed_values(meta, totals, params, convs, voxel_mask, base):
    return pl.pallas_call(
        normed_kernel,
        name="normed_values",
        out_shape=jax.ShapeDtypeStruct((16, 16, CHANS, DEPTH), BF16),
        in_specs=[SMEM, VMEM, VMEM, HBM, VMEM, HBM],
        out_specs=HBM,
        scratch_shapes=[
            pltpu.VMEM(BLOCKS, F32),
            pltpu.VMEM(BLOCKS, BF16),
            pltpu.SemaphoreType.DMA((SLOTS, BRICK)),
            pltpu.SemaphoreType.DMA((SLOTS, BRICK)),
        ],
        input_output_aliases={5: 0},
        compiler_params=params_of(12),
        cost_estimate=cost(30_000_000, 8_000_000),
    )(meta, totals, params, convs, voxel_mask, base)


def weight_kernel(meta, field, slope, out, acc):
    acc[...] = jnp.zeros(acc.shape, F32)
    lane = lax.broadcasted_iota(jnp.int32, (CHANS, DEPTH), 1)

    def row(slot, x):
        x0, y0 = corner(meta, slot)
        shifted = [[], [], []]
        for col in range(BRICK):
            here = slope[x0 + x + 1, y0 + col + 1]
            wide = here.astype(F32)
            shifted[0].append(
                jnp.where(lane == DEPTH - 1, 0.0, pltpu.roll(wide, DEPTH - 1, 1)).astype(BF16)
            )
            shifted[1].append(here)
            shifted[2].append(jnp.where(lane == 0, 0.0, pltpu.roll(wide, 1, 1)).astype(BF16))
        left = jnp.concatenate([jnp.concatenate(s, axis=1) for s in shifted], axis=0)
        right = []
        for a in range(3):
            for b in range(3):
                cols = [field[x0 + x + a, y0 + b + col] for col in range(BRICK)]
                right.append(jnp.concatenate(cols, axis=1))
        right.append(jnp.zeros((COLS - 9 * CHANS, BRICK * DEPTH), BF16))
        acc[...] += lax.dot_general(
            left,
            jnp.concatenate(right, axis=0),
            (((1,), (1,)), ((), ())),
            preferred_element_type=F32,
        )

    each_row(meta[8], row, unroll=2)
    for tile in range(TILES):
        out[ROWS * tile : ROWS * (tile + 1)] = acc[:, DEPTH * tile : DEPTH * (tile + 1)]
    out[ROWS * TILES :] = jnp.zeros((2048 - ROWS * TILES, DEPTH), F32)


def weight_terms(meta, field, slope):
    return pl.pallas_call(
        weight_kernel,
        name="weight_terms",
        out_shape=jax.ShapeDtypeStruct((2048, DEPTH), F32),
        in_specs=[SMEM, VMEM, VMEM],
        out_specs=VMEM,
        scratch_shapes=[pltpu.VMEM((ROWS, COLS), F32)],
        compiler_params=params_of(4),
        cost_estimate=cost(16_000_000_000, 2_000_000),
    )(meta, field, slope)


def share_kernel(parts, out):
    mine = jnp.sum(parts[...], axis=0).astype(BF16)
    out[...] = jnp.broadcast_to(mine[None], out.shape)


def share(parts):
    return pl.pallas_call(
        share_kernel,
        name="share",
        out_shape=jax.ShapeDtypeStruct((DEVICES, 16, DEPTH), BF16),
        in_specs=[VMEM],
        out_specs=VMEM,
        compiler_params=params_of(2),
        cost_estimate=cost(300_000, 1_500_000),
    )(parts)


def arrange_kernel(flat, out):
    tiles = [flat[ROWS * t : ROWS * (t + 1)].astype(F32) for t in range(TILES)]
    for plane in range(9):
        tile, shift = CHANS * plane // DEPTH, CHANS * plane % DEPTH
        both = jnp.concatenate([tiles[tile], tiles[min(tile + 1, TILES - 1)]], axis=1)
        if shift:
            both = pltpu.roll(both, 2 * DEPTH - shift, 1)
        for e in range(3):
            out[3 * plane + e] = both[CHANS * e : CHANS * (e + 1), 0:CHANS]


def arrange(flat):
    return pl.pallas_call(
        arrange_kernel,
        name="arrange",
        out_shape=jax.ShapeDtypeStruct((27, CHANS, CHANS), F32),
        in_specs=[VMEM],
        out_specs=VMEM,
        compiler_params=params_of(4),
        cost_estimate=cost(300_000, 1_500_000),
    )(flat)


def backward_kernel(
    meta, kept, mask, xm, xp, ym, yp, taps, base, out, field, results, sem_rim, sem_in, sem_out
):
    occupied = meta[8]
    for slot in range(4):
        x0, y0 = corner(meta, slot)

        if slot < SLOTS:

            @pl.when(slot < occupied)
            def _():
                pltpu.make_async_copy(
                    kept.at[slot],
                    field.at[pl.ds(x0 + 1, BRICK), pl.ds(y0 + 1, BRICK)],
                    sem_in.at[slot],
                ).start()

    rims = fill_rims(meta, field, (xm, xp, ym, yp), sem_rim)
    clear_pillars(meta, field)
    for copy in rims:
        copy.wait()
    for slot in range(SLOTS):
        x0, y0 = corner(meta, slot)

        @pl.when(slot < occupied)
        def _():
            pltpu.make_async_copy(
                kept.at[slot],
                field.at[pl.ds(x0 + 1, BRICK), pl.ds(y0 + 1, BRICK)],
                sem_in.at[slot],
            ).wait()

    def copy(slot, x):
        x0, y0 = corner(meta, slot)
        return pltpu.make_async_copy(
            results.at[slot, x], out.at[x0 + x, pl.ds(y0, BRICK)], sem_out.at[slot, x]
        )

    def row(slot, x):
        x0, y0 = corner(meta, slot)
        active = active_rows(mask, x0 + x, y0)
        outs = column_convs(field, taps, x0 + x, y0, True)
        for col in range(BRICK):
            results[slot, x, col] = (outs[col] * active[col : col + 1]).astype(BF16)
        copy(slot, x).start()

    each_row(occupied, row, unroll=2)
    each_row(occupied, lambda slot, x: copy(slot, x).wait())


def backward(meta, kept, voxel_mask, rims, taps, base):
    return pl.pallas_call(
        backward_kernel,
        name="backward",
        out_shape=jax.ShapeDtypeStruct((16, 16, CHANS, DEPTH), BF16),
        in_specs=[SMEM, HBM, VMEM, ANY, ANY, ANY, ANY, VMEM, HBM],
        out_specs=HBM,
        scratch_shapes=[
            pltpu.VMEM(FIELD, BF16),
            pltpu.VMEM(BLOCKS, BF16),
            pltpu.SemaphoreType.DMA((4,)),
            pltpu.SemaphoreType.DMA((SLOTS,)),
            pltpu.SemaphoreType.DMA((SLOTS, BRICK)),
        ],
        input_output_aliases={8: 0},
        compiler_params=params_of(15),
        cost_estimate=cost(16_000_000_000, 5_000_000),
    )(meta, kept, voxel_mask, *rims, taps, base)


def corner_kernel(stride, meta, *refs):
    x_even, x_odd, even, odd, sems = refs[-5:]
    x_end, y_end = near_ends(meta)
    copies = []
    for target, line in ((even, 15 * y_end), (odd, 15 - 15 * y_end)):
        for source, end in ((x_even, x_end), (x_odd, 1 - x_end)):
            copies.append(
                pltpu.make_async_copy(
                    source.at[line], target.at[stride * end], sems.at[len(copies)]
                )
            )
    for copy in copies:
        copy.start()
    for copy in copies:
        copy.wait()


def corners_of(meta, x_even, x_odd):
    pair = jax.ShapeDtypeStruct((2, CHANS, DEPTH), BF16)
    return pl.pallas_call(
        functools.partial(corner_kernel, 1),
        name="corners",
        out_shape=(pair, pair),
        in_specs=[SMEM, ANY, ANY],
        out_specs=(ANY, ANY),
        scratch_shapes=[pltpu.SemaphoreType.DMA((4,))],
        compiler_params=params_of(1),
        cost_estimate=cost(1_000, 200_000),
    )(meta, x_even, x_odd)


def stitch(meta, y_even, y_odd, x_even, x_odd):
    return pl.pallas_call(
        functools.partial(corner_kernel, 17),
        name="stitch",
        out_shape=(LONG, LONG),
        in_specs=[SMEM, ANY, ANY, ANY, ANY],
        out_specs=(ANY, ANY),
        scratch_shapes=[pltpu.SemaphoreType.DMA((4,))],
        input_output_aliases={1: 0, 2: 1},
        compiler_params=params_of(1),
        cost_estimate=cost(1_000, 200_000),
    )(meta, y_even, y_odd, x_even, x_odd)


def taps_kernel(weight, ahead, back):
    lane = lax.broadcasted_iota(jnp.int32, (CHANS, DEPTH), 1)
    side = jnp.zeros((CHANS, DEPTH - CHANS), F32)
    wide = [jnp.concatenate([weight[t].astype(F32), side], axis=1) for t in range(27)]
    below = jnp.zeros((DEPTH - CHANS, DEPTH), F32)

    def pack(blocks):
        tiles = []
        for tile in range(TILES):
            value = jnp.zeros((CHANS, DEPTH), F32)
            for place, block in enumerate(blocks):
                start = CHANS * place - DEPTH * tile
                if start >= DEPTH or start + CHANS <= 0:
                    continue
                moved = pltpu.roll(block, start % DEPTH, 1) if start % DEPTH else block
                here = jnp.logical_and(lane >= start, lane < start + CHANS)
                value = jnp.where(here, moved, value)
            tiles.append(value)
        return jnp.concatenate(tiles, axis=1).astype(BF16)

    for e in range(3):
        rows = slice(CHANS * e, CHANS * (e + 1))
        ahead[rows] = pack([wide[3 * plane + e] for plane in range(9)])
        turned = [
            jnp.transpose(jnp.concatenate([wide[3 * plane + e], below], axis=0))[0:CHANS]
            for plane in reversed(range(9))
        ]
        back[rows] = pack(turned)


def tap_kernels(weight):
    packed = jax.ShapeDtypeStruct((ROWS, COLS), BF16)
    return pl.pallas_call(
        taps_kernel,
        name="tap_kernels",
        out_shape=(packed, packed),
        in_specs=[VMEM],
        out_specs=(VMEM, VMEM),
        compiler_params=params_of(6),
        cost_estimate=cost(1_000_000, 2_000_000),
    )(weight)


def exchange(even, odd, axis):
    count = lax.axis_size(axis)
    meets = [(i, i + 1) for i in range(1, count - 1, 2)]
    return (
        lax.ppermute(even, axis, [(i, i ^ 1) for i in range(count)]),
        lax.ppermute(odd, axis, meets + [(j, i) for i, j in meets]),
    )


def swap_all(pieces):
    return lax.all_to_all(pieces, ("slab", "sub"), 0, 0, tiled=True)


def body(features, voxel_mask, weight, norm_gain, norm_bias, out_grad):
    x_even, x_odd, y_even, y_odd, meta = prepare(features, voxel_mask)
    x_rims = exchange(x_even, x_odd, "slab")
    y_rims = exchange(y_even, y_odd, "sub")
    field = build(meta, features, voxel_mask)
    ahead, back = tap_kernels(weight)
    params = jnp.pad(jnp.stack([norm_gain, norm_bias]), ((0, 6), (0, DEPTH - CHANS)))
    x_rims, field, ahead, back, params = lax.optimization_barrier(
        (x_rims, field, ahead, back, params)
    )
    corners = exchange(*corners_of(meta, *x_rims), "sub")
    rims = (*x_rims, *y_rims, *corners)
    conv, stats = forward(meta, field, out_grad, voxel_mask, rims, ahead)
    slope, kept, x_even, x_odd, y_even, y_odd, sums, totals = slopes(
        meta, swap_all(stats), params, conv, out_grad, voxel_mask
    )
    x_rims = exchange(x_even, x_odd, "slab")
    rims, x_even = lax.optimization_barrier((rims, x_even))
    field = build(meta, features, voxel_mask, rims)
    normed_base, feature_base = blanks(meta)
    x_rims, slope, field, normed_base, feature_base = lax.optimization_barrier(
        (x_rims, slope, field, normed_base, feature_base)
    )
    y_rims = exchange(*stitch(meta, y_even, y_odd, *x_rims), "sub")
    terms = weight_terms(meta, field, slope)
    parts = swap_all(terms.reshape(DEVICES, 16, DEPTH))
    normed_out = normed_values(meta, totals, params, conv, voxel_mask, normed_base)
    shared = swap_all(share(parts))
    feature_grad = backward(meta, kept, voxel_mask, (*x_rims, *y_rims), back, feature_base)
    weight_grad = arrange(shared.reshape(2048, DEPTH))
    return (normed_out, feature_grad, weight_grad, sums[0, :CHANS], sums[1, :CHANS])


def solution(mesh):
    placed = (
        P("slab", "sub", None, None),
        P("slab", "sub", None),
        P(),
        P(),
        P(),
        P("slab", "sub", None, None),
    )
    return jax.shard_map(
        body,
        mesh=mesh,
        in_specs=placed,
        out_specs=(P("slab", "sub", None, None), P("slab", "sub", None, None), P(), P(), P()),
        check_vma=False,
    )
```

```python
import functools

import jax
import jax.numpy as jnp
from jax import lax
from jax.experimental import pallas as pl
from jax.experimental.pallas import tpu as pltpu
from jax.sharding import PartitionSpec as P

BRICK = 8
SLOTS = 2
EPSILON = 1e-05
DEVICES = 128
CHANS = 96
DEPTH = 128
TILES = 7
ROWS = 3 * CHANS
COLS = TILES * DEPTH
F32 = jnp.float32
BF16 = jnp.bfloat16
FIELD = (18, 18, CHANS, DEPTH)
BLOCKS = (SLOTS, BRICK, BRICK, CHANS, DEPTH)
MIB = 1024 * 1024
WIDE_CONVS = (24,) + BLOCKS[1:]
WIDE_SLOPES = (48,) + BLOCKS[1:]

ANY = pl.BlockSpec(memory_space=pl.ANY)
VMEM = pl.BlockSpec(memory_space=pltpu.VMEM)
SMEM = pl.BlockSpec(memory_space=pltpu.SMEM)
HBM = pl.BlockSpec(memory_space=pltpu.HBM)


def params_of(mib, **more):
    return pltpu.CompilerParams(vmem_limit_bytes=mib * MIB, **more)


def cost(flops, moved):
    return pl.CostEstimate(flops=flops, bytes_accessed=moved, transcendentals=0)


def corner(meta, slot):
    return (pl.multiple_of(meta[2 * slot], BRICK), pl.multiple_of(meta[2 * slot + 1], BRICK))


def active_rows(mask, x, y0):
    return mask[x, pl.ds(y0, BRICK), :].astype(F32)


def each_row(occupied, step, unroll=1):
    for slot in range(SLOTS):

        @pl.when(slot < occupied)
        def _():
            lax.fori_loop(
                0, BRICK, lambda x, carry: (step(slot, x), carry)[1], 0, unroll=unroll
            )


def clear_pillars(meta, field):
    for slot in range(4):

        @pl.when(slot >= meta[8])
        def _():
            x0, y0 = corner(meta, slot)

            def clear(row, carry):
                for col in range(BRICK):
                    field[x0 + row + 1, y0 + col + 1] = jnp.zeros((CHANS, DEPTH), BF16)
                return carry

            lax.fori_loop(0, BRICK, clear, 0)


def near_ends(meta):
    return 1 - meta[9], 1 - meta[10]


def fill_rims(meta, field, rims, sems):
    x_end, y_end = near_ends(meta)
    side = pl.ds(1, 16) if len(rims) > 4 else pl.ds(0, 18)
    copies = []
    for turn in range(2):
        row = 17 * (x_end if turn == 0 else 1 - x_end)
        col = 17 * (y_end if turn == 0 else 1 - y_end)
        moves = [
            (rims[turn], field.at[row, pl.ds(1, 16)]),
            (rims[2 + turn], field.at[side, col]),
        ]
        if len(rims) > 4:
            moves += [(rims[4 + turn].at[end], field.at[17 * end, col]) for end in range(2)]
        for source, target in moves:
            copies.append(pltpu.make_async_copy(source, target, sems.at[len(copies)]))
    for copy in copies:
        copy.start()
    return copies


def take_rims(meta, field, rims, sems):
    x_end, y_end = near_ends(meta)
    inner = pl.ds(1, 16)
    copies = []
    for turn in range(2):
        row = 1 + 15 * (x_end if turn == 0 else 1 - x_end)
        col = 1 + 15 * (y_end if turn == 0 else 1 - y_end)
        copies += [
            pltpu.make_async_copy(field.at[row, inner], rims[turn], sems.at[turn]),
            pltpu.make_async_copy(
                field.at[inner, col], rims[2 + turn].at[inner], sems.at[2 + turn]
            ),
        ]
    for copy in copies:
        copy.start()
    for copy in copies:
        copy.wait()


RIM = jax.ShapeDtypeStruct((16, CHANS, DEPTH), BF16)
LONG = jax.ShapeDtypeStruct((18, CHANS, DEPTH), BF16)


def prepare_kernel(features, mask, x_even, x_odd, y_even, y_odd, meta, sem_in):
    faces, sides = (x_even, x_odd), (y_even, y_odd)
    meta[9] = lax.axis_index("core")
    meta[10] = lax.rem(lax.axis_index("sub"), 2)
    x_end, y_end = near_ends(meta)
    rows, cols = (15 * x_end, 15 - 15 * x_end), (15 * y_end, 15 - 15 * y_end)
    loads = [
        pltpu.make_async_copy(features.at[rows[0]], x_even, sem_in.at[0]),
        pltpu.make_async_copy(features.at[rows[1]], x_odd, sem_in.at[1]),
        pltpu.make_async_copy(features.at[:, cols[0]], y_even, sem_in.at[2]),
        pltpu.make_async_copy(features.at[:, cols[1]], y_odd, sem_in.at[3]),
    ]
    for load in loads:
        load.start()

    flags = []
    for px in range(2):
        for py in range(2):
            cells = mask[BRICK * px : BRICK * (px + 1), BRICK * py : BRICK * (py + 1), :]
            flags.append(jnp.max(cells))
    taken = jnp.int32(0)
    for flag in flags:
        taken = taken + flag
    meta[8] = taken
    full, free = jnp.int32(0), taken
    for place, flag in enumerate(flags):
        rank = jnp.where(flag == 1, full, free)
        meta[2 * rank] = jnp.int32(place // 2 * BRICK)
        meta[2 * rank + 1] = jnp.int32(place % 2 * BRICK)
        full = full + flag
        free = free + 1 - flag

    for which in range(2):
        loads[which].wait()
        for col in range(16):
            keep = jnp.broadcast_to(mask[rows[which], col : col + 1, :], (CHANS, DEPTH))
            faces[which][col] = faces[which][col] * keep.astype(F32).astype(BF16)
    for which in range(2):
        loads[2 + which].wait()
        for row in range(16):
            keep = jnp.broadcast_to(mask[row, pl.ds(cols[which], 1), :], (CHANS, DEPTH))
            sides[which][row] = sides[which][row] * keep.astype(F32).astype(BF16)


def prepare(features, voxel_mask):
    return pl.pallas_call(
        prepare_kernel,
        name="prepare",
        out_shape=(RIM, RIM, RIM, RIM, jax.ShapeDtypeStruct((11,), jnp.int32)),
        in_specs=[HBM, VMEM],
        out_specs=(VMEM, VMEM, VMEM, VMEM, SMEM),
        scratch_shapes=[pltpu.SemaphoreType.DMA((4,))],
        compiler_params=params_of(54),
        cost_estimate=cost(3_000_000, 3_000_000),
    )(features, voxel_mask)


def build_kernel(meta, features, mask, *refs):
    *rims, field, sem_rim = refs
    copies = fill_rims(meta, field, rims, sem_rim) if rims else []

    def mask_row(slot, x):
        x0, y0 = corner(meta, slot)
        active = active_rows(mask, x0 + x, y0)
        for col in range(BRICK):
            keep = jnp.broadcast_to(active[col : col + 1], (CHANS, DEPTH)).astype(BF16)
            field[x0 + x + 1, y0 + col + 1] = features[x0 + x, y0 + col] * keep

    clear_pillars(meta, field)
    each_row(meta[8], mask_row)
    for copy in copies:
        copy.wait()


def build(meta, features, voxel_mask, rims=()):
    return pl.pallas_call(
        build_kernel,
        name="build_whole" if rims else "build",
        out_shape=jax.ShapeDtypeStruct(FIELD, BF16),
        in_specs=[SMEM, VMEM, VMEM] + [ANY] * len(rims),
        out_specs=VMEM,
        scratch_shapes=[pltpu.SemaphoreType.DMA((8,))],
        compiler_params=params_of(2),
        cost_estimate=cost(3_000_000, 6_000_000),
    )(meta, features, voxel_mask, *rims)


def column_convs(field, kernel_ref, x, y0, flipped):
    lane = lax.broadcasted_iota(jnp.int32, (CHANS, DEPTH), 1)
    up, down = (2, 0) if flipped else (0, 2)
    outs = []
    for pair in range(BRICK // 2):
        pieces = []
        for a in range(3):
            for b in range(3):
                col = y0 + 2 * pair + b
                pieces.append(jnp.concatenate([field[x + a, col], field[x + a, col + 1]], axis=1))
        pieces.append(jnp.zeros((COLS - 9 * CHANS, 2 * DEPTH), BF16))
        planes = jnp.dot(
            kernel_ref[...], jnp.concatenate(pieces, axis=0), preferred_element_type=F32
        )
        for half in range(2):
            part = [
                planes[CHANS * e : CHANS * (e + 1), DEPTH * half : DEPTH * (half + 1)]
                for e in range(3)
            ]
            outs.append(
                part[1]
                + jnp.where(lane == 0, 0.0, pltpu.roll(part[up], 1, 1))
                + jnp.where(lane == DEPTH - 1, 0.0, pltpu.roll(part[down], DEPTH - 1, 1))
            )
    return outs


def forward_kernel(
    meta, before, grads, mask, xm, xp, ym, yp, cm, cp, taps, field, conv_out, stats, convs, sums, sem_rim, sem_out
):
    def conv_copy(slot, x):
        return pltpu.make_async_copy(convs.at[slot, x], conv_out.at[slot, x], sem_out.at[slot, x])

    rims = fill_rims(meta, field, (xm, xp, ym, yp, cm, cp), sem_rim)
    for copy in rims:
        copy.wait()
    sums[...] = jnp.zeros(sums.shape, F32)

    def row(slot, x):
        x0, y0 = corner(meta, slot)
        active = active_rows(mask, x0 + x, y0)
        outs = column_convs(field, taps, x0 + x, y0, False)
        total, square, upsum, cross = [sums[k] for k in range(4)]
        for col in range(BRICK):
            keep = active[col : col + 1]
            conv = outs[col] * keep
            convs[slot, x, col] = conv
            up = grads[x0 + x, y0 + col].astype(F32) * keep
            total = total + conv
            square = square + conv * conv
            upsum = upsum + up
            cross = cross + up * conv
        for k, value in enumerate((total, square, upsum, cross)):
            sums[k] = value
        sums[4, 0:BRICK] = sums[4, 0:BRICK] + active
        conv_copy(slot, x).start()

    each_row(meta[8], row, unroll=4)

    ones = jnp.ones((8, DEPTH), F32)
    rows = []
    for k in range(5):
        flat = lax.dot_general(
            ones,
            sums[k],
            (((1,), (1,)), ((), ())),
            precision=lax.Precision.HIGHEST,
            preferred_element_type=F32,
        )
        rows.append(flat[0:1])
    rows.append(jnp.zeros((3, CHANS), F32))
    packed = jnp.concatenate(
        [jnp.concatenate(rows, axis=0), jnp.zeros((8, DEPTH - CHANS), F32)], axis=1
    )
    stats[...] = jnp.broadcast_to(packed[None], stats.shape)
    each_row(meta[8], lambda slot, x: conv_copy(slot, x).wait())


def forward(meta, field, out_grad, voxel_mask, rims, taps):
    return pl.pallas_call(
        forward_kernel,
        name="forward",
        out_shape=(
            jax.ShapeDtypeStruct(FIELD, BF16),
            jax.ShapeDtypeStruct(WIDE_CONVS, F32),
            jax.ShapeDtypeStruct((DEVICES, 8, DEPTH), F32),
        ),
        in_specs=[SMEM, VMEM, VMEM, VMEM] + [ANY] * 6 + [VMEM],
        out_specs=(VMEM, HBM, VMEM),
        scratch_shapes=[
            pltpu.VMEM(BLOCKS, F32),
            pltpu.VMEM((5, CHANS, DEPTH), F32),
            pltpu.SemaphoreType.DMA((8,)),
            pltpu.SemaphoreType.DMA((SLOTS, BRICK)),
        ],
        input_output_aliases={1: 0},
        compiler_params=params_of(10),
        cost_estimate=cost(16_000_000_000, 4_000_000),
    )(meta, field, out_grad, voxel_mask, *rims, taps)[1:]


def spread(row):
    return jnp.transpose(jnp.broadcast_to(row, (DEPTH, DEPTH)))[0:CHANS]


def blank_kernel(meta, normed, feature, blank, sems):
    occupied = meta[8]

    def clear(x, carry):
        for col in range(BRICK):
            blank[x, col] = jnp.zeros((CHANS, DEPTH), BF16)
        return carry

    lax.fori_loop(0, BRICK, clear, 0)

    def copies(slot):
        x0, y0 = corner(meta, slot)
        spot = (pl.ds(x0, BRICK), pl.ds(y0, BRICK))
        return (
            pltpu.make_async_copy(blank, normed.at[spot], sems.at[slot, 0]),
            pltpu.make_async_copy(blank, feature.at[spot], sems.at[slot, 1]),
        )

    for slot in range(4):

        @pl.when(slot >= occupied)
        def _():
            for copy in copies(slot):
                copy.start()

    for slot in range(4):

        @pl.when(slot >= occupied)
        def _():
            for copy in copies(slot):
                copy.wait()


def blanks(meta):
    dense = jax.ShapeDtypeStruct((16, 16, CHANS, DEPTH), BF16)
    return pl.pallas_call(
        blank_kernel,
        name="blanks",
        out_shape=(dense, dense),
        in_specs=[SMEM],
        out_specs=(HBM, HBM),
        scratch_shapes=[
            pltpu.VMEM((BRICK, BRICK, CHANS, DEPTH), BF16),
            pltpu.SemaphoreType.DMA((4, 2)),
        ],
        compiler_params=params_of(3),
        cost_estimate=cost(1_000, 8_000_000),
    )(meta)


def norm_rows(totals):
    total, square, upsum, cross = [totals[k : k + 1] for k in range(4)]
    count = jnp.sum(totals[4:5])
    mean = total / count
    inv_std = lax.rsqrt(square / count - mean * mean + EPSILON)
    return count, mean, inv_std, upsum, cross


def slope_kernel(
    meta, gathered, params, conv, grads, mask, field, kept, x_even, x_odd, y_even, y_odd, sums_out, totals_out, convs, sem_conv, sem_kept, sem_rim
):
    occupied = meta[8]

    def load(slot, x):
        return pltpu.make_async_copy(conv.at[slot, x], convs.at[slot, x], sem_conv.at[slot, x])

    each_row(occupied, lambda slot, x: load(slot, x).start())

    def keep_row(slot, x):
        x0, y0 = corner(meta, slot)
        return pltpu.make_async_copy(
            field.at[x0 + x + 1, pl.ds(y0 + 1, BRICK)], kept.at[slot, x], sem_kept.at[slot, x]
        )

    clear_pillars(meta, field)
    totals = jnp.sum(gathered[...], axis=0)
    totals_out[...] = totals
    count, mean, inv_std, upsum, cross = norm_rows(totals)
    gain_grad = inv_std * (cross - mean * upsum)
    sums_out[...] = jnp.zeros(sums_out.shape, F32)
    sums_out[0:1] = gain_grad
    sums_out[1:2] = upsum
    mean_c, inv_c = spread(mean), spread(inv_std)
    up_c, cross_c = spread(upsum / count), spread(gain_grad / count)
    scale_c = spread(params[0:1] * inv_std)

    def row(slot, x):
        x0, y0 = corner(meta, slot)
        load(slot, x).wait()
        active = active_rows(mask, x0 + x, y0)
        for col in range(BRICK):
            keep = active[col : col + 1]
            normed = (convs[slot, x, col] - mean_c) * inv_c
            up = grads[x0 + x, y0 + col].astype(F32)
            field[x0 + x + 1, y0 + col + 1] = (
                scale_c * (up - up_c - normed * cross_c) * keep
            ).astype(BF16)
        keep_row(slot, x).start()

    each_row(occupied, row, unroll=2)
    take_rims(meta, field, (x_even, x_odd, y_even, y_odd), sem_rim)
    each_row(occupied, lambda slot, x: keep_row(slot, x).wait())


def slopes(meta, gathered, params, conv, out_grad, voxel_mask):
    small = jax.ShapeDtypeStruct((8, DEPTH), F32)
    kept = jax.ShapeDtypeStruct(WIDE_SLOPES, BF16)
    return pl.pallas_call(
        slope_kernel,
        name="slopes",
        out_shape=(jax.ShapeDtypeStruct(FIELD, BF16), kept, RIM, RIM, LONG, LONG, small, small),
        in_specs=[SMEM, VMEM, VMEM, HBM, VMEM, VMEM],
        out_specs=(VMEM, HBM, ANY, ANY, ANY, ANY, VMEM, VMEM),
        scratch_shapes=[
            pltpu.VMEM(BLOCKS, F32),
            pltpu.SemaphoreType.DMA((SLOTS, BRICK)),
            pltpu.SemaphoreType.DMA((SLOTS, BRICK)),
            pltpu.SemaphoreType.DMA((4,)),
        ],
        compiler_params=params_of(9),
        cost_estimate=cost(30_000_000, 12_000_000),
    )(meta, gathered, params, conv, out_grad, voxel_mask)


def normed_kernel(meta, totals, params, conv, mask, base, out, convs, ys, sem_conv, sems):
    def load(slot, x):
        return pltpu.make_async_copy(conv.at[slot, x], convs.at[slot, x], sem_conv.at[slot, x])

    each_row(meta[8], lambda slot, x: load(slot, x).start())
    _, mean, inv_std, _, _ = norm_rows(totals)
    mean_c, inv_c = spread(mean), spread(inv_std)
    gain_c, bias_c = spread(params[0:1]), spread(params[1:2])

    def copy(slot, x):
        x0, y0 = corner(meta, slot)
        return pltpu.make_async_copy(
            ys.at[slot, x], out.at[x0 + x, pl.ds(y0, BRICK)], sems.at[slot, x]
        )

    def row(slot, x):
        x0, y0 = corner(meta, slot)
        active = active_rows(mask, x0 + x, y0)
        load(slot, x).wait()
        for col in range(BRICK):
            normed = (convs[slot, x, col] - mean_c) * inv_c
            ys[slot, x, col] = ((gain_c * normed + bias_c) * active[col : col + 1]).astype(BF16)
        copy(slot, x).start()

    each_row(meta[8], row, unroll=2)
    each_row(meta[8], lambda slot, x: copy(slot, x).wait())


def normed_values(meta, totals, params, convs, voxel_mask, base):
    return pl.pallas_call(
        normed_kernel,
        name="normed_values",
        out_shape=jax.ShapeDtypeStruct((16, 16, CHANS, DEPTH), BF16),
        in_specs=[SMEM, VMEM, VMEM, HBM, VMEM, HBM],
        out_specs=HBM,
        scratch_shapes=[
            pltpu.VMEM(BLOCKS, F32),
            pltpu.VMEM(BLOCKS, BF16),
            pltpu.SemaphoreType.DMA((SLOTS, BRICK)),
            pltpu.SemaphoreType.DMA((SLOTS, BRICK)),
        ],
        input_output_aliases={5: 0},
        compiler_params=params_of(12),
        cost_estimate=cost(30_000_000, 8_000_000),
    )(meta, totals, params, convs, voxel_mask, base)


def weight_kernel(meta, field, slope, mine, other, acc, out):
    acc[...] = jnp.zeros(acc.shape, F32)
    lane = lax.broadcasted_iota(jnp.int32, (CHANS, DEPTH), 1)

    def row(slot, x):
        x0, y0 = corner(meta, slot)
        shifted = [[], [], []]
        for col in range(BRICK):
            here = slope[x0 + x + 1, y0 + col + 1]
            wide = here.astype(F32)
            shifted[0].append(
                jnp.where(lane == DEPTH - 1, 0.0, pltpu.roll(wide, DEPTH - 1, 1)).astype(BF16)
            )
            shifted[1].append(here)
            shifted[2].append(jnp.where(lane == 0, 0.0, pltpu.roll(wide, 1, 1)).astype(BF16))
        left = jnp.concatenate([jnp.concatenate(s, axis=1) for s in shifted], axis=0)
        right = []
        for a in range(3):
            for b in range(3):
                cols = [field[x0 + x + a, y0 + b + col] for col in range(BRICK)]
                right.append(jnp.concatenate(cols, axis=1))
        right.append(jnp.zeros((COLS - 9 * CHANS, BRICK * DEPTH), BF16))
        acc[...] += lax.dot_general(
            left,
            jnp.concatenate(right, axis=0),
            (((1,), (1,)), ((), ())),
            preferred_element_type=F32,
        )

    each_row(meta[8], row, unroll=4)
    for tile in range(TILES):
        out[ROWS * tile : ROWS * (tile + 1)] = acc[:, DEPTH * tile : DEPTH * (tile + 1)]
    out[ROWS * TILES :] = jnp.zeros((2048 - ROWS * TILES, DEPTH), F32)
    for pair in range(16):
        for target, core in ((mine, meta[9]), (other, 1 - meta[9])):
            start = pl.multiple_of(128 * pair + 64 * core, 64)
            target[pair] = out[pl.ds(start, 64)]


def weight_terms(meta, field, slope):
    half = jax.ShapeDtypeStruct((16, 64, DEPTH), F32)
    return pl.pallas_call(
        weight_kernel,
        name="weight_terms",
        out_shape=(half, half),
        in_specs=[SMEM, VMEM, VMEM],
        out_specs=(VMEM, VMEM),
        scratch_shapes=[pltpu.VMEM((ROWS, COLS), F32), pltpu.VMEM((2048, DEPTH), F32)],
        compiler_params=params_of(6),
        cost_estimate=cost(16_000_000_000, 2_000_000),
    )(meta, field, slope)


def share_kernel(parts, out):
    mine = jnp.sum(parts[...], axis=0).astype(BF16)
    out[...] = jnp.broadcast_to(mine[None], out.shape)


def share(parts):
    return pl.pallas_call(
        share_kernel,
        name="share",
        out_shape=jax.ShapeDtypeStruct((DEVICES, 16, DEPTH), BF16),
        in_specs=[VMEM],
        out_specs=VMEM,
        compiler_params=params_of(2),
        cost_estimate=cost(300_000, 1_500_000),
    )(parts)


def arrange_kernel(flat, out):
    tiles = [flat[ROWS * t : ROWS * (t + 1)].astype(F32) for t in range(TILES)]
    for plane in range(9):
        tile, shift = CHANS * plane // DEPTH, CHANS * plane % DEPTH
        both = jnp.concatenate([tiles[tile], tiles[min(tile + 1, TILES - 1)]], axis=1)
        if shift:
            both = pltpu.roll(both, 2 * DEPTH - shift, 1)
        for e in range(3):
            out[3 * plane + e] = both[CHANS * e : CHANS * (e + 1), 0:CHANS]


def arrange(flat):
    return pl.pallas_call(
        arrange_kernel,
        name="arrange",
        out_shape=jax.ShapeDtypeStruct((27, CHANS, CHANS), F32),
        in_specs=[VMEM],
        out_specs=VMEM,
        compiler_params=params_of(4),
        cost_estimate=cost(300_000, 1_500_000),
    )(flat)


def backward_kernel(
    meta, kept, mask, xm, xp, ym, yp, taps, base, out, field, results, sem_rim, sem_in, sem_out
):
    occupied = meta[8]
    for slot in range(4):
        x0, y0 = corner(meta, slot)

        if slot < SLOTS:

            @pl.when(slot < occupied)
            def _():
                pltpu.make_async_copy(
                    kept.at[slot],
                    field.at[pl.ds(x0 + 1, BRICK), pl.ds(y0 + 1, BRICK)],
                    sem_in.at[slot],
                ).start()

    rims = fill_rims(meta, field, (xm, xp, ym, yp), sem_rim)
    clear_pillars(meta, field)
    for copy in rims:
        copy.wait()
    for slot in range(SLOTS):
        x0, y0 = corner(meta, slot)

        @pl.when(slot < occupied)
        def _():
            pltpu.make_async_copy(
                kept.at[slot],
                field.at[pl.ds(x0 + 1, BRICK), pl.ds(y0 + 1, BRICK)],
                sem_in.at[slot],
            ).wait()

    def copy(slot, x):
        x0, y0 = corner(meta, slot)
        return pltpu.make_async_copy(
            results.at[slot, x], out.at[x0 + x, pl.ds(y0, BRICK)], sem_out.at[slot, x]
        )

    def row(slot, x):
        x0, y0 = corner(meta, slot)
        active = active_rows(mask, x0 + x, y0)
        outs = column_convs(field, taps, x0 + x, y0, True)
        for col in range(BRICK):
            results[slot, x, col] = (outs[col] * active[col : col + 1]).astype(BF16)
        copy(slot, x).start()

    each_row(occupied, row, unroll=4)
    each_row(occupied, lambda slot, x: copy(slot, x).wait())


def backward(meta, kept, voxel_mask, rims, taps, base):
    return pl.pallas_call(
        backward_kernel,
        name="backward",
        out_shape=jax.ShapeDtypeStruct((16, 16, CHANS, DEPTH), BF16),
        in_specs=[SMEM, HBM, VMEM, ANY, ANY, ANY, ANY, VMEM, HBM],
        out_specs=HBM,
        scratch_shapes=[
            pltpu.VMEM(FIELD, BF16),
            pltpu.VMEM(BLOCKS, BF16),
            pltpu.SemaphoreType.DMA((4,)),
            pltpu.SemaphoreType.DMA((SLOTS,)),
            pltpu.SemaphoreType.DMA((SLOTS, BRICK)),
        ],
        input_output_aliases={8: 0},
        compiler_params=params_of(15),
        cost_estimate=cost(16_000_000_000, 5_000_000),
    )(meta, kept, voxel_mask, *rims, taps, base)


def corner_kernel(stride, meta, *refs):
    x_even, x_odd, even, odd, sems = refs[-5:]
    x_end, y_end = near_ends(meta)
    copies = []
    for target, line in ((even, 15 * y_end), (odd, 15 - 15 * y_end)):
        for source, end in ((x_even, x_end), (x_odd, 1 - x_end)):
            copies.append(
                pltpu.make_async_copy(
                    source.at[line], target.at[stride * end], sems.at[len(copies)]
                )
            )
    for copy in copies:
        copy.start()
    for copy in copies:
        copy.wait()


def corners_of(meta, x_even, x_odd):
    pair = jax.ShapeDtypeStruct((2, CHANS, DEPTH), BF16)
    return pl.pallas_call(
        functools.partial(corner_kernel, 1),
        name="corners",
        out_shape=(pair, pair),
        in_specs=[SMEM, ANY, ANY],
        out_specs=(ANY, ANY),
        scratch_shapes=[pltpu.SemaphoreType.DMA((4,))],
        compiler_params=params_of(1),
        cost_estimate=cost(1_000, 200_000),
    )(meta, x_even, x_odd)


def stitch(meta, y_even, y_odd, x_even, x_odd):
    return pl.pallas_call(
        functools.partial(corner_kernel, 17),
        name="stitch",
        out_shape=(LONG, LONG),
        in_specs=[SMEM, ANY, ANY, ANY, ANY],
        out_specs=(ANY, ANY),
        scratch_shapes=[pltpu.SemaphoreType.DMA((4,))],
        input_output_aliases={1: 0, 2: 1},
        compiler_params=params_of(1),
        cost_estimate=cost(1_000, 200_000),
    )(meta, y_even, y_odd, x_even, x_odd)


def taps_kernel(weight, ahead, back):
    lane = lax.broadcasted_iota(jnp.int32, (CHANS, DEPTH), 1)
    side = jnp.zeros((CHANS, DEPTH - CHANS), F32)
    wide = [jnp.concatenate([weight[t].astype(F32), side], axis=1) for t in range(27)]
    below = jnp.zeros((DEPTH - CHANS, DEPTH), F32)

    def pack(blocks):
        tiles = []
        for tile in range(TILES):
            value = jnp.zeros((CHANS, DEPTH), F32)
            for place, block in enumerate(blocks):
                start = CHANS * place - DEPTH * tile
                if start >= DEPTH or start + CHANS <= 0:
                    continue
                moved = pltpu.roll(block, start % DEPTH, 1) if start % DEPTH else block
                here = jnp.logical_and(lane >= start, lane < start + CHANS)
                value = jnp.where(here, moved, value)
            tiles.append(value)
        return jnp.concatenate(tiles, axis=1).astype(BF16)

    for e in range(3):
        rows = slice(CHANS * e, CHANS * (e + 1))
        ahead[rows] = pack([wide[3 * plane + e] for plane in range(9)])
        turned = [
            jnp.transpose(jnp.concatenate([wide[3 * plane + e], below], axis=0))[0:CHANS]
            for plane in reversed(range(9))
        ]
        back[rows] = pack(turned)


def tap_kernels(weight):
    packed = jax.ShapeDtypeStruct((ROWS, COLS), BF16)
    return pl.pallas_call(
        taps_kernel,
        name="tap_kernels",
        out_shape=(packed, packed),
        in_specs=[VMEM],
        out_specs=(VMEM, VMEM),
        compiler_params=params_of(6),
        cost_estimate=cost(1_000_000, 2_000_000),
    )(weight)


def exchange(even, odd, axis, count):
    meets = [(i, i + 1) for i in range(1, count - 1, 2)]
    return (
        lax.ppermute(even, axis, [(i, i ^ 1) for i in range(count)]),
        lax.ppermute(odd, axis, meets + [(j, i) for i, j in meets]),
    )


def swap_all(pieces):
    return lax.all_to_all(pieces, ("pair", "core", "sub"), 0, 0, tiled=True)


def reduce_pieces(mine, other):
    half = mine + lax.ppermute(other, "core", [(0, 1), (1, 0)])
    pieces = half.reshape(DEVICES // 2, 16, DEPTH)
    return lax.all_to_all(pieces, ("pair", "sub"), 0, 0, tiled=True)


def body(features, voxel_mask, weight, norm_gain, norm_bias, out_grad):
    slabs, subs = lax.axis_size("pair") * 2, lax.axis_size("sub")
    x_even, x_odd, y_even, y_odd, meta = prepare(features, voxel_mask)
    x_rims = exchange(x_even, x_odd, ("pair", "core"), slabs)
    y_rims = exchange(y_even, y_odd, "sub", subs)
    field = build(meta, features, voxel_mask)
    ahead, back = tap_kernels(weight)
    params = jnp.pad(jnp.stack([norm_gain, norm_bias]), ((0, 6), (0, DEPTH - CHANS)))
    x_rims, field, ahead, back, params = lax.optimization_barrier(
        (x_rims, field, ahead, back, params)
    )
    corners = exchange(*corners_of(meta, *x_rims), "sub", subs)
    rims = (*x_rims, *y_rims, *corners)
    conv, stats = forward(meta, field, out_grad, voxel_mask, rims, ahead)
    slope, kept, x_even, x_odd, y_even, y_odd, sums, totals = slopes(
        meta, swap_all(stats), params, conv, out_grad, voxel_mask
    )
    x_rims = exchange(x_even, x_odd, ("pair", "core"), slabs)
    rims, x_even = lax.optimization_barrier((rims, x_even))
    field = build(meta, features, voxel_mask, rims)
    normed_base, feature_base = blanks(meta)
    x_rims, slope, field, normed_base, feature_base = lax.optimization_barrier(
        (x_rims, slope, field, normed_base, feature_base)
    )
    y_rims = exchange(*stitch(meta, y_even, y_odd, *x_rims), "sub", subs)
    parts = reduce_pieces(*weight_terms(meta, field, slope))
    normed_out = normed_values(meta, totals, params, conv, voxel_mask, normed_base)
    shared = swap_all(share(parts))
    feature_grad = backward(meta, kept, voxel_mask, (*x_rims, *y_rims), back, feature_base)
    weight_grad = arrange(shared.reshape(2048, DEPTH))
    return (normed_out, feature_grad, weight_grad, sums[0, :CHANS], sums[1, :CHANS])


def solution(mesh):
    slabs, subs = mesh.devices.shape
    paired = jax.sharding.Mesh(
        mesh.devices.reshape(slabs // 2, 2, subs), ("pair", "core", "sub")
    )
    slab = ("pair", "core")
    placed = (
        P(slab, "sub", None, None),
        P(slab, "sub", None),
        P(),
        P(),
        P(),
        P(slab, "sub", None, None),
    )
    return jax.shard_map(
        body,
        mesh=paired,
        in_specs=placed,
        out_specs=(P(slab, "sub", None, None), P(slab, "sub", None, None), P(), P(), P()),
        check_vma=False,
    )
```

```python
import functools

import jax
import jax.numpy as jnp
from jax import lax
from jax.experimental import pallas as pl
from jax.experimental.pallas import tpu as pltpu
from jax.sharding import PartitionSpec as P

BRICK = 8
SLOTS = 2
EPSILON = 1e-05
DEVICES = 128
CHANS = 96
DEPTH = 128
TILES = 7
ROWS = 3 * CHANS
COLS = TILES * DEPTH
F32 = jnp.float32
BF16 = jnp.bfloat16
FIELD = (18, 18, CHANS, DEPTH)
BLOCKS = (SLOTS, BRICK, BRICK, CHANS, DEPTH)
MIB = 1024 * 1024
WIDE_CONVS = (24,) + BLOCKS[1:]
WIDE_SLOPES = (48,) + BLOCKS[1:]

ANY = pl.BlockSpec(memory_space=pl.ANY)
VMEM = pl.BlockSpec(memory_space=pltpu.VMEM)
SMEM = pl.BlockSpec(memory_space=pltpu.SMEM)
HBM = pl.BlockSpec(memory_space=pltpu.HBM)


def params_of(mib, **more):
    return pltpu.CompilerParams(vmem_limit_bytes=mib * MIB, **more)


def cost(flops, moved):
    return pl.CostEstimate(flops=flops, bytes_accessed=moved, transcendentals=0)


def corner(meta, slot):
    return (pl.multiple_of(meta[2 * slot], BRICK), pl.multiple_of(meta[2 * slot + 1], BRICK))


def active_rows(mask, x, y0):
    return mask[x, pl.ds(y0, BRICK), :].astype(F32)


def each_row(occupied, step, unroll=1):
    for slot in range(SLOTS):

        @pl.when(slot < occupied)
        def _():
            lax.fori_loop(
                0, BRICK, lambda x, carry: (step(slot, x), carry)[1], 0, unroll=unroll
            )


def clear_pillars(meta, field):
    for slot in range(4):

        @pl.when(slot >= meta[8])
        def _():
            x0, y0 = corner(meta, slot)

            def clear(row, carry):
                for col in range(BRICK):
                    field[x0 + row + 1, y0 + col + 1] = jnp.zeros((CHANS, DEPTH), BF16)
                return carry

            lax.fori_loop(0, BRICK, clear, 0)


def near_ends(meta):
    return 1 - meta[9], 1 - meta[10]


def fill_rims(meta, field, rims, sems):
    x_end, y_end = near_ends(meta)
    side = pl.ds(1, 16) if len(rims) > 4 else pl.ds(0, 18)
    copies = []
    for turn in range(2):
        row = 17 * (x_end if turn == 0 else 1 - x_end)
        col = 17 * (y_end if turn == 0 else 1 - y_end)
        moves = [
            (rims[turn], field.at[row, pl.ds(1, 16)]),
            (rims[2 + turn], field.at[side, col]),
        ]
        if len(rims) > 4:
            moves += [(rims[4 + turn].at[end], field.at[17 * end, col]) for end in range(2)]
        for source, target in moves:
            copies.append(pltpu.make_async_copy(source, target, sems.at[len(copies)]))
    for copy in copies:
        copy.start()
    return copies


def take_rims(meta, field, rims, sems):
    x_end, y_end = near_ends(meta)
    inner = pl.ds(1, 16)
    copies = []
    for turn in range(2):
        row = 1 + 15 * (x_end if turn == 0 else 1 - x_end)
        col = 1 + 15 * (y_end if turn == 0 else 1 - y_end)
        copies += [
            pltpu.make_async_copy(field.at[row, inner], rims[turn], sems.at[turn]),
            pltpu.make_async_copy(
                field.at[inner, col], rims[2 + turn].at[inner], sems.at[2 + turn]
            ),
        ]
    for copy in copies:
        copy.start()
    for copy in copies:
        copy.wait()


RIM = jax.ShapeDtypeStruct((16, CHANS, DEPTH), BF16)
LONG = jax.ShapeDtypeStruct((18, CHANS, DEPTH), BF16)


def prepare_kernel(features, mask, x_even, x_odd, y_even, y_odd, meta, sem_in):
    faces, sides = (x_even, x_odd), (y_even, y_odd)
    meta[9] = lax.axis_index("core")
    meta[10] = lax.rem(lax.axis_index("sub"), 2)
    x_end, y_end = near_ends(meta)
    rows, cols = (15 * x_end, 15 - 15 * x_end), (15 * y_end, 15 - 15 * y_end)
    loads = [
        pltpu.make_async_copy(features.at[rows[0]], x_even, sem_in.at[0]),
        pltpu.make_async_copy(features.at[rows[1]], x_odd, sem_in.at[1]),
        pltpu.make_async_copy(features.at[:, cols[0]], y_even, sem_in.at[2]),
        pltpu.make_async_copy(features.at[:, cols[1]], y_odd, sem_in.at[3]),
    ]
    for load in loads:
        load.start()

    flags = []
    for px in range(2):
        for py in range(2):
            cells = mask[BRICK * px : BRICK * (px + 1), BRICK * py : BRICK * (py + 1), :]
            flags.append(jnp.max(cells))
    taken = jnp.int32(0)
    for flag in flags:
        taken = taken + flag
    meta[8] = taken
    full, free = jnp.int32(0), taken
    for place, flag in enumerate(flags):
        rank = jnp.where(flag == 1, full, free)
        meta[2 * rank] = jnp.int32(place // 2 * BRICK)
        meta[2 * rank + 1] = jnp.int32(place % 2 * BRICK)
        full = full + flag
        free = free + 1 - flag

    for which in range(2):
        loads[which].wait()
        for col in range(16):
            keep = jnp.broadcast_to(mask[rows[which], col : col + 1, :], (CHANS, DEPTH))
            faces[which][col] = faces[which][col] * keep.astype(F32).astype(BF16)
    for which in range(2):
        loads[2 + which].wait()
        for row in range(16):
            keep = jnp.broadcast_to(mask[row, pl.ds(cols[which], 1), :], (CHANS, DEPTH))
            sides[which][row] = sides[which][row] * keep.astype(F32).astype(BF16)


def prepare(features, voxel_mask):
    return pl.pallas_call(
        prepare_kernel,
        name="prepare",
        out_shape=(RIM, RIM, RIM, RIM, jax.ShapeDtypeStruct((11,), jnp.int32)),
        in_specs=[HBM, VMEM],
        out_specs=(VMEM, VMEM, VMEM, VMEM, SMEM),
        scratch_shapes=[pltpu.SemaphoreType.DMA((4,))],
        compiler_params=params_of(54),
        cost_estimate=cost(3_000_000, 3_000_000),
    )(features, voxel_mask)


def build_kernel(meta, features, mask, *refs):
    *rims, field, sem_rim = refs
    copies = fill_rims(meta, field, rims, sem_rim) if rims else []

    def mask_row(slot, x):
        x0, y0 = corner(meta, slot)
        active = active_rows(mask, x0 + x, y0)
        for col in range(BRICK):
            keep = jnp.broadcast_to(active[col : col + 1], (CHANS, DEPTH)).astype(BF16)
            field[x0 + x + 1, y0 + col + 1] = features[x0 + x, y0 + col] * keep

    clear_pillars(meta, field)
    each_row(meta[8], mask_row)
    for copy in copies:
        copy.wait()


def build(meta, features, voxel_mask, rims=()):
    return pl.pallas_call(
        build_kernel,
        name="build_whole" if rims else "build",
        out_shape=jax.ShapeDtypeStruct(FIELD, BF16),
        in_specs=[SMEM, VMEM, VMEM] + [ANY] * len(rims),
        out_specs=VMEM,
        scratch_shapes=[pltpu.SemaphoreType.DMA((8,))],
        compiler_params=params_of(2),
        cost_estimate=cost(3_000_000, 6_000_000),
    )(meta, features, voxel_mask, *rims)


def column_convs(field, kernel_ref, x, y0, flipped):
    lane = lax.broadcasted_iota(jnp.int32, (CHANS, DEPTH), 1)
    up, down = (2, 0) if flipped else (0, 2)
    outs = []
    for pair in range(BRICK // 2):
        pieces = []
        for a in range(3):
            for b in range(3):
                col = y0 + 2 * pair + b
                pieces.append(jnp.concatenate([field[x + a, col], field[x + a, col + 1]], axis=1))
        pieces.append(jnp.zeros((COLS - 9 * CHANS, 2 * DEPTH), BF16))
        planes = jnp.dot(
            kernel_ref[...], jnp.concatenate(pieces, axis=0), preferred_element_type=F32
        )
        for half in range(2):
            part = [
                planes[CHANS * e : CHANS * (e + 1), DEPTH * half : DEPTH * (half + 1)]
                for e in range(3)
            ]
            outs.append(
                part[1]
                + jnp.where(lane == 0, 0.0, pltpu.roll(part[up], 1, 1))
                + jnp.where(lane == DEPTH - 1, 0.0, pltpu.roll(part[down], DEPTH - 1, 1))
            )
    return outs


def forward_kernel(
    meta, before, grads, mask, xm, xp, ym, yp, cm, cp, taps, field, conv_out, stats, convs, sums, sem_rim, sem_out
):
    def conv_copy(slot, x):
        return pltpu.make_async_copy(convs.at[slot, x], conv_out.at[slot, x], sem_out.at[slot, x])

    rims = fill_rims(meta, field, (xm, xp, ym, yp, cm, cp), sem_rim)
    for copy in rims:
        copy.wait()
    sums[...] = jnp.zeros(sums.shape, F32)

    def row(slot, x):
        x0, y0 = corner(meta, slot)
        active = active_rows(mask, x0 + x, y0)
        outs = column_convs(field, taps, x0 + x, y0, False)
        total, square, upsum, cross = [sums[k] for k in range(4)]
        for col in range(BRICK):
            keep = active[col : col + 1]
            conv = outs[col] * keep
            convs[slot, x, col] = conv
            up = grads[x0 + x, y0 + col].astype(F32) * keep
            total = total + conv
            square = square + conv * conv
            upsum = upsum + up
            cross = cross + up * conv
        for k, value in enumerate((total, square, upsum, cross)):
            sums[k] = value
        sums[4, 0:BRICK] = sums[4, 0:BRICK] + active
        conv_copy(slot, x).start()

    each_row(meta[8], row, unroll=8)

    ones = jnp.ones((8, DEPTH), F32)
    rows = []
    for k in range(5):
        flat = lax.dot_general(
            ones,
            sums[k],
            (((1,), (1,)), ((), ())),
            precision=lax.Precision.HIGHEST,
            preferred_element_type=F32,
        )
        rows.append(flat[0:1])
    rows.append(jnp.zeros((3, CHANS), F32))
    packed = jnp.concatenate(
        [jnp.concatenate(rows, axis=0), jnp.zeros((8, DEPTH - CHANS), F32)], axis=1
    )
    stats[...] = jnp.broadcast_to(packed[None], stats.shape)
    each_row(meta[8], lambda slot, x: conv_copy(slot, x).wait())


def forward(meta, field, out_grad, voxel_mask, rims, taps):
    return pl.pallas_call(
        forward_kernel,
        name="forward",
        out_shape=(
            jax.ShapeDtypeStruct(FIELD, BF16),
            jax.ShapeDtypeStruct(WIDE_CONVS, F32),
            jax.ShapeDtypeStruct((DEVICES, 8, DEPTH), F32),
        ),
        in_specs=[SMEM, VMEM, VMEM, VMEM] + [ANY] * 6 + [VMEM],
        out_specs=(VMEM, HBM, VMEM),
        scratch_shapes=[
            pltpu.VMEM(BLOCKS, F32),
            pltpu.VMEM((5, CHANS, DEPTH), F32),
            pltpu.SemaphoreType.DMA((8,)),
            pltpu.SemaphoreType.DMA((SLOTS, BRICK)),
        ],
        input_output_aliases={1: 0},
        compiler_params=params_of(10),
        cost_estimate=cost(16_000_000_000, 4_000_000),
    )(meta, field, out_grad, voxel_mask, *rims, taps)[1:]


def spread(row):
    return jnp.transpose(jnp.broadcast_to(row, (DEPTH, DEPTH)))[0:CHANS]


def blank_kernel(meta, normed, feature, blank, sems):
    occupied = meta[8]

    def clear(x, carry):
        for col in range(BRICK):
            blank[x, col] = jnp.zeros((CHANS, DEPTH), BF16)
        return carry

    lax.fori_loop(0, BRICK, clear, 0)

    def copies(slot):
        x0, y0 = corner(meta, slot)
        spot = (pl.ds(x0, BRICK), pl.ds(y0, BRICK))
        return (
            pltpu.make_async_copy(blank, normed.at[spot], sems.at[slot, 0]),
            pltpu.make_async_copy(blank, feature.at[spot], sems.at[slot, 1]),
        )

    for slot in range(4):

        @pl.when(slot >= occupied)
        def _():
            for copy in copies(slot):
                copy.start()

    for slot in range(4):

        @pl.when(slot >= occupied)
        def _():
            for copy in copies(slot):
                copy.wait()


def blanks(meta):
    dense = jax.ShapeDtypeStruct((16, 16, CHANS, DEPTH), BF16)
    return pl.pallas_call(
        blank_kernel,
        name="blanks",
        out_shape=(dense, dense),
        in_specs=[SMEM],
        out_specs=(HBM, HBM),
        scratch_shapes=[
            pltpu.VMEM((BRICK, BRICK, CHANS, DEPTH), BF16),
            pltpu.SemaphoreType.DMA((4, 2)),
        ],
        compiler_params=params_of(3),
        cost_estimate=cost(1_000, 8_000_000),
    )(meta)


def norm_rows(totals):
    total, square, upsum, cross = [totals[k : k + 1] for k in range(4)]
    count = jnp.sum(totals[4:5])
    mean = total / count
    inv_std = lax.rsqrt(square / count - mean * mean + EPSILON)
    return count, mean, inv_std, upsum, cross


def slope_kernel(
    meta, gathered, params, conv, grads, mask, field, kept, x_even, x_odd, y_even, y_odd, sums_out, totals_out, convs, sem_conv, sem_kept, sem_rim
):
    occupied = meta[8]

    def load(slot, x):
        return pltpu.make_async_copy(conv.at[slot, x], convs.at[slot, x], sem_conv.at[slot, x])

    each_row(occupied, lambda slot, x: load(slot, x).start())

    def keep_row(slot, x):
        x0, y0 = corner(meta, slot)
        return pltpu.make_async_copy(
            field.at[x0 + x + 1, pl.ds(y0 + 1, BRICK)], kept.at[slot, x], sem_kept.at[slot, x]
        )

    clear_pillars(meta, field)
    totals = jnp.sum(gathered[...], axis=0)
    totals_out[...] = totals
    count, mean, inv_std, upsum, cross = norm_rows(totals)
    gain_grad = inv_std * (cross - mean * upsum)
    sums_out[...] = jnp.zeros(sums_out.shape, F32)
    sums_out[0:1] = gain_grad
    sums_out[1:2] = upsum
    mean_c, inv_c = spread(mean), spread(inv_std)
    up_c, cross_c = spread(upsum / count), spread(gain_grad / count)
    scale_c = spread(params[0:1] * inv_std)

    def row(slot, x):
        x0, y0 = corner(meta, slot)
        load(slot, x).wait()
        active = active_rows(mask, x0 + x, y0)
        for col in range(BRICK):
            keep = active[col : col + 1]
            normed = (convs[slot, x, col] - mean_c) * inv_c
            up = grads[x0 + x, y0 + col].astype(F32)
            field[x0 + x + 1, y0 + col + 1] = (
                scale_c * (up - up_c - normed * cross_c) * keep
            ).astype(BF16)
        keep_row(slot, x).start()

    each_row(occupied, row, unroll=4)
    take_rims(meta, field, (x_even, x_odd, y_even, y_odd), sem_rim)
    each_row(occupied, lambda slot, x: keep_row(slot, x).wait())


def slopes(meta, gathered, params, conv, out_grad, voxel_mask):
    small = jax.ShapeDtypeStruct((8, DEPTH), F32)
    kept = jax.ShapeDtypeStruct(WIDE_SLOPES, BF16)
    return pl.pallas_call(
        slope_kernel,
        name="slopes",
        out_shape=(jax.ShapeDtypeStruct(FIELD, BF16), kept, RIM, RIM, LONG, LONG, small, small),
        in_specs=[SMEM, VMEM, VMEM, HBM, VMEM, VMEM],
        out_specs=(VMEM, HBM, ANY, ANY, ANY, ANY, VMEM, VMEM),
        scratch_shapes=[
            pltpu.VMEM(BLOCKS, F32),
            pltpu.SemaphoreType.DMA((SLOTS, BRICK)),
            pltpu.SemaphoreType.DMA((SLOTS, BRICK)),
            pltpu.SemaphoreType.DMA((4,)),
        ],
        compiler_params=params_of(9),
        cost_estimate=cost(30_000_000, 12_000_000),
    )(meta, gathered, params, conv, out_grad, voxel_mask)


def normed_kernel(meta, totals, params, conv, mask, base, out, convs, ys, sem_conv, sems):
    def load(slot, x):
        return pltpu.make_async_copy(conv.at[slot, x], convs.at[slot, x], sem_conv.at[slot, x])

    each_row(meta[8], lambda slot, x: load(slot, x).start())
    _, mean, inv_std, _, _ = norm_rows(totals)
    mean_c, inv_c = spread(mean), spread(inv_std)
    gain_c, bias_c = spread(params[0:1]), spread(params[1:2])

    def copy(slot, x):
        x0, y0 = corner(meta, slot)
        return pltpu.make_async_copy(
            ys.at[slot, x], out.at[x0 + x, pl.ds(y0, BRICK)], sems.at[slot, x]
        )

    def row(slot, x):
        x0, y0 = corner(meta, slot)
        active = active_rows(mask, x0 + x, y0)
        load(slot, x).wait()
        for col in range(BRICK):
            normed = (convs[slot, x, col] - mean_c) * inv_c
            ys[slot, x, col] = ((gain_c * normed + bias_c) * active[col : col + 1]).astype(BF16)
        copy(slot, x).start()

    each_row(meta[8], row, unroll=4)
    each_row(meta[8], lambda slot, x: copy(slot, x).wait())


def normed_values(meta, totals, params, convs, voxel_mask, base):
    return pl.pallas_call(
        normed_kernel,
        name="normed_values",
        out_shape=jax.ShapeDtypeStruct((16, 16, CHANS, DEPTH), BF16),
        in_specs=[SMEM, VMEM, VMEM, HBM, VMEM, HBM],
        out_specs=HBM,
        scratch_shapes=[
            pltpu.VMEM(BLOCKS, F32),
            pltpu.VMEM(BLOCKS, BF16),
            pltpu.SemaphoreType.DMA((SLOTS, BRICK)),
            pltpu.SemaphoreType.DMA((SLOTS, BRICK)),
        ],
        input_output_aliases={5: 0},
        compiler_params=params_of(12),
        cost_estimate=cost(30_000_000, 8_000_000),
    )(meta, totals, params, convs, voxel_mask, base)


def weight_kernel(meta, field, slope, mine, other, acc, out):
    acc[...] = jnp.zeros(acc.shape, F32)
    lane = lax.broadcasted_iota(jnp.int32, (CHANS, DEPTH), 1)

    def row(slot, x):
        x0, y0 = corner(meta, slot)
        shifted = [[], [], []]
        for col in range(BRICK):
            here = slope[x0 + x + 1, y0 + col + 1]
            wide = here.astype(F32)
            shifted[0].append(
                jnp.where(lane == DEPTH - 1, 0.0, pltpu.roll(wide, DEPTH - 1, 1)).astype(BF16)
            )
            shifted[1].append(here)
            shifted[2].append(jnp.where(lane == 0, 0.0, pltpu.roll(wide, 1, 1)).astype(BF16))
        left = jnp.concatenate([jnp.concatenate(s, axis=1) for s in shifted], axis=0)
        right = []
        for a in range(3):
            for b in range(3):
                cols = [field[x0 + x + a, y0 + b + col] for col in range(BRICK)]
                right.append(jnp.concatenate(cols, axis=1))
        right.append(jnp.zeros((COLS - 9 * CHANS, BRICK * DEPTH), BF16))
        acc[...] += lax.dot_general(
            left,
            jnp.concatenate(right, axis=0),
            (((1,), (1,)), ((), ())),
            preferred_element_type=F32,
        )

    each_row(meta[8], row, unroll=8)
    for tile in range(TILES):
        out[ROWS * tile : ROWS * (tile + 1)] = acc[:, DEPTH * tile : DEPTH * (tile + 1)]
    out[ROWS * TILES :] = jnp.zeros((2048 - ROWS * TILES, DEPTH), F32)
    for pair in range(16):
        for target, core in ((mine, meta[9]), (other, 1 - meta[9])):
            start = pl.multiple_of(128 * pair + 64 * core, 64)
            target[pair] = out[pl.ds(start, 64)]


def weight_terms(meta, field, slope):
    half = jax.ShapeDtypeStruct((16, 64, DEPTH), F32)
    return pl.pallas_call(
        weight_kernel,
        name="weight_terms",
        out_shape=(half, half),
        in_specs=[SMEM, VMEM, VMEM],
        out_specs=(VMEM, VMEM),
        scratch_shapes=[pltpu.VMEM((ROWS, COLS), F32), pltpu.VMEM((2048, DEPTH), F32)],
        compiler_params=params_of(6),
        cost_estimate=cost(16_000_000_000, 2_000_000),
    )(meta, field, slope)


def share_kernel(parts, out):
    mine = jnp.sum(parts[...], axis=0).astype(BF16)
    out[...] = jnp.broadcast_to(mine[None], out.shape)


def share(parts):
    return pl.pallas_call(
        share_kernel,
        name="share",
        out_shape=jax.ShapeDtypeStruct((DEVICES, 16, DEPTH), BF16),
        in_specs=[VMEM],
        out_specs=VMEM,
        compiler_params=params_of(2),
        cost_estimate=cost(300_000, 1_500_000),
    )(parts)


def arrange_kernel(flat, out):
    tiles = [flat[ROWS * t : ROWS * (t + 1)].astype(F32) for t in range(TILES)]
    for plane in range(9):
        tile, shift = CHANS * plane // DEPTH, CHANS * plane % DEPTH
        both = jnp.concatenate([tiles[tile], tiles[min(tile + 1, TILES - 1)]], axis=1)
        if shift:
            both = pltpu.roll(both, 2 * DEPTH - shift, 1)
        for e in range(3):
            out[3 * plane + e] = both[CHANS * e : CHANS * (e + 1), 0:CHANS]


def arrange(flat):
    return pl.pallas_call(
        arrange_kernel,
        name="arrange",
        out_shape=jax.ShapeDtypeStruct((27, CHANS, CHANS), F32),
        in_specs=[VMEM],
        out_specs=VMEM,
        compiler_params=params_of(4),
        cost_estimate=cost(300_000, 1_500_000),
    )(flat)


def backward_kernel(
    meta, kept, mask, xm, xp, ym, yp, taps, base, out, field, results, sem_rim, sem_in, sem_out
):
    occupied = meta[8]
    for slot in range(4):
        x0, y0 = corner(meta, slot)

        if slot < SLOTS:

            @pl.when(slot < occupied)
            def _():
                pltpu.make_async_copy(
                    kept.at[slot],
                    field.at[pl.ds(x0 + 1, BRICK), pl.ds(y0 + 1, BRICK)],
                    sem_in.at[slot],
                ).start()

    rims = fill_rims(meta, field, (xm, xp, ym, yp), sem_rim)
    clear_pillars(meta, field)
    for copy in rims:
        copy.wait()
    for slot in range(SLOTS):
        x0, y0 = corner(meta, slot)

        @pl.when(slot < occupied)
        def _():
            pltpu.make_async_copy(
                kept.at[slot],
                field.at[pl.ds(x0 + 1, BRICK), pl.ds(y0 + 1, BRICK)],
                sem_in.at[slot],
            ).wait()

    def copy(slot, x):
        x0, y0 = corner(meta, slot)
        return pltpu.make_async_copy(
            results.at[slot, x], out.at[x0 + x, pl.ds(y0, BRICK)], sem_out.at[slot, x]
        )

    def row(slot, x):
        x0, y0 = corner(meta, slot)
        active = active_rows(mask, x0 + x, y0)
        outs = column_convs(field, taps, x0 + x, y0, True)
        for col in range(BRICK):
            results[slot, x, col] = (outs[col] * active[col : col + 1]).astype(BF16)
        copy(slot, x).start()

    each_row(occupied, row, unroll=8)
    each_row(occupied, lambda slot, x: copy(slot, x).wait())


def backward(meta, kept, voxel_mask, rims, taps, base):
    return pl.pallas_call(
        backward_kernel,
        name="backward",
        out_shape=jax.ShapeDtypeStruct((16, 16, CHANS, DEPTH), BF16),
        in_specs=[SMEM, HBM, VMEM, ANY, ANY, ANY, ANY, VMEM, HBM],
        out_specs=HBM,
        scratch_shapes=[
            pltpu.VMEM(FIELD, BF16),
            pltpu.VMEM(BLOCKS, BF16),
            pltpu.SemaphoreType.DMA((4,)),
            pltpu.SemaphoreType.DMA((SLOTS,)),
            pltpu.SemaphoreType.DMA((SLOTS, BRICK)),
        ],
        input_output_aliases={8: 0},
        compiler_params=params_of(15),
        cost_estimate=cost(16_000_000_000, 5_000_000),
    )(meta, kept, voxel_mask, *rims, taps, base)


def corner_kernel(stride, meta, *refs):
    x_even, x_odd, even, odd, sems = refs[-5:]
    x_end, y_end = near_ends(meta)
    copies = []
    for target, line in ((even, 15 * y_end), (odd, 15 - 15 * y_end)):
        for source, end in ((x_even, x_end), (x_odd, 1 - x_end)):
            copies.append(
                pltpu.make_async_copy(
                    source.at[line], target.at[stride * end], sems.at[len(copies)]
                )
            )
    for copy in copies:
        copy.start()
    for copy in copies:
        copy.wait()


def corners_of(meta, x_even, x_odd):
    pair = jax.ShapeDtypeStruct((2, CHANS, DEPTH), BF16)
    return pl.pallas_call(
        functools.partial(corner_kernel, 1),
        name="corners",
        out_shape=(pair, pair),
        in_specs=[SMEM, ANY, ANY],
        out_specs=(ANY, ANY),
        scratch_shapes=[pltpu.SemaphoreType.DMA((4,))],
        compiler_params=params_of(1),
        cost_estimate=cost(1_000, 200_000),
    )(meta, x_even, x_odd)


def stitch(meta, y_even, y_odd, x_even, x_odd):
    return pl.pallas_call(
        functools.partial(corner_kernel, 17),
        name="stitch",
        out_shape=(LONG, LONG),
        in_specs=[SMEM, ANY, ANY, ANY, ANY],
        out_specs=(ANY, ANY),
        scratch_shapes=[pltpu.SemaphoreType.DMA((4,))],
        input_output_aliases={1: 0, 2: 1},
        compiler_params=params_of(1),
        cost_estimate=cost(1_000, 200_000),
    )(meta, y_even, y_odd, x_even, x_odd)


def taps_kernel(weight, ahead, back):
    lane = lax.broadcasted_iota(jnp.int32, (CHANS, DEPTH), 1)
    side = jnp.zeros((CHANS, DEPTH - CHANS), F32)
    wide = [jnp.concatenate([weight[t].astype(F32), side], axis=1) for t in range(27)]
    below = jnp.zeros((DEPTH - CHANS, DEPTH), F32)

    def pack(blocks):
        tiles = []
        for tile in range(TILES):
            value = jnp.zeros((CHANS, DEPTH), F32)
            for place, block in enumerate(blocks):
                start = CHANS * place - DEPTH * tile
                if start >= DEPTH or start + CHANS <= 0:
                    continue
                moved = pltpu.roll(block, start % DEPTH, 1) if start % DEPTH else block
                here = jnp.logical_and(lane >= start, lane < start + CHANS)
                value = jnp.where(here, moved, value)
            tiles.append(value)
        return jnp.concatenate(tiles, axis=1).astype(BF16)

    for e in range(3):
        rows = slice(CHANS * e, CHANS * (e + 1))
        ahead[rows] = pack([wide[3 * plane + e] for plane in range(9)])
        turned = [
            jnp.transpose(jnp.concatenate([wide[3 * plane + e], below], axis=0))[0:CHANS]
            for plane in reversed(range(9))
        ]
        back[rows] = pack(turned)


def tap_kernels(weight):
    packed = jax.ShapeDtypeStruct((ROWS, COLS), BF16)
    return pl.pallas_call(
        taps_kernel,
        name="tap_kernels",
        out_shape=(packed, packed),
        in_specs=[VMEM],
        out_specs=(VMEM, VMEM),
        compiler_params=params_of(6),
        cost_estimate=cost(1_000_000, 2_000_000),
    )(weight)


def exchange(even, odd, axis, count):
    meets = [(i, i + 1) for i in range(1, count - 1, 2)]
    return (
        lax.ppermute(even, axis, [(i, i ^ 1) for i in range(count)]),
        lax.ppermute(odd, axis, meets + [(j, i) for i, j in meets]),
    )


def swap_all(pieces):
    return lax.all_to_all(pieces, ("pair", "core", "sub"), 0, 0, tiled=True)


def reduce_pieces(mine, other):
    half = mine + lax.ppermute(other, "core", [(0, 1), (1, 0)])
    pieces = half.reshape(DEVICES // 2, 16, DEPTH)
    return lax.all_to_all(pieces, ("pair", "sub"), 0, 0, tiled=True)


def body(features, voxel_mask, weight, norm_gain, norm_bias, out_grad):
    slabs, subs = lax.axis_size("pair") * 2, lax.axis_size("sub")
    x_even, x_odd, y_even, y_odd, meta = prepare(features, voxel_mask)
    x_rims = exchange(x_even, x_odd, ("pair", "core"), slabs)
    y_rims = exchange(y_even, y_odd, "sub", subs)
    field = build(meta, features, voxel_mask)
    ahead, back = tap_kernels(weight)
    params = jnp.pad(jnp.stack([norm_gain, norm_bias]), ((0, 6), (0, DEPTH - CHANS)))
    x_rims, field, ahead, back, params = lax.optimization_barrier(
        (x_rims, field, ahead, back, params)
    )
    corners = exchange(*corners_of(meta, *x_rims), "sub", subs)
    rims = (*x_rims, *y_rims, *corners)
    conv, stats = forward(meta, field, out_grad, voxel_mask, rims, ahead)
    slope, kept, x_even, x_odd, y_even, y_odd, sums, totals = slopes(
        meta, swap_all(stats), params, conv, out_grad, voxel_mask
    )
    x_rims = exchange(x_even, x_odd, ("pair", "core"), slabs)
    rims, x_even = lax.optimization_barrier((rims, x_even))
    field = build(meta, features, voxel_mask, rims)
    normed_base, feature_base = blanks(meta)
    x_rims, slope, field, normed_base, feature_base = lax.optimization_barrier(
        (x_rims, slope, field, normed_base, feature_base)
    )
    y_rims = exchange(*stitch(meta, y_even, y_odd, *x_rims), "sub", subs)
    parts = reduce_pieces(*weight_terms(meta, field, slope))
    normed_out = normed_values(meta, totals, params, conv, voxel_mask, normed_base)
    shared = swap_all(share(parts))
    feature_grad = backward(meta, kept, voxel_mask, (*x_rims, *y_rims), back, feature_base)
    weight_grad = arrange(shared.reshape(2048, DEPTH))
    return (normed_out, feature_grad, weight_grad, sums[0, :CHANS], sums[1, :CHANS])


def solution(mesh):
    slabs, subs = mesh.devices.shape
    paired = jax.sharding.Mesh(
        mesh.devices.reshape(slabs // 2, 2, subs), ("pair", "core", "sub")
    )
    slab = ("pair", "core")
    placed = (
        P(slab, "sub", None, None),
        P(slab, "sub", None),
        P(),
        P(),
        P(),
        P(slab, "sub", None, None),
    )
    return jax.shard_map(
        body,
        mesh=paired,
        in_specs=placed,
        out_specs=(P(slab, "sub", None, None), P(slab, "sub", None, None), P(), P(), P()),
        check_vma=False,
    )
```
